128 devices in a mesh: row: 16 (over y_hi, z, core), col: 4 (over x), rep: 2 (over y_lo).
Axes of the slice: x: 4, y: 4 (y_hi: 2, y_lo: 2; y = y_hi * 2 + y_lo), z: 4, core: 2. Of those that a mesh axis runs over, the one named last changes fastest.
Arguments:
- activations: bfloat16 [2, 2048, 8192], P('rep', 'row', 'col'), may hold values from -6 to 6
- out_grads: bfloat16 [2, 2048, 26624], P('rep', 'col', 'row'), may hold values from -0.1875 to 0.1875
- weight_code: bfloat16 [8192, 26624], P(('col', 'rep'), 'row'), may hold values from -1 to 1
- weight_scale: float32 [64, 208], P(('col', 'rep'), 'row'), may hold values from 0.005 to 0.05
- moment_code: bfloat16 [8192, 26624], P(('col', 'rep'), 'row'), may hold values from -1 to 1
- moment_scale: float32 [64, 208], P(('col', 'rep'), 'row'), may hold values from 0.05 to 0.5
- second_code: bfloat16 [8192, 26624], P(('col', 'rep'), 'row'), may hold values from 0.049804688 to 1
- second_scale: float32 [64, 208], P(('col', 'rep'), 'row'), may hold values from 0.05 to 1
Outputs:
- new_weight: bfloat16 [8192, 26624], P('col', 'row')
- new_weight_scale: float32 [64, 208], P('col', 'row')
- new_moment: bfloat16 [8192, 26624], P(('col', 'rep'), 'row')
- new_moment_scale: float32 [64, 208], P(('col', 'rep'), 'row')
- new_second: bfloat16 [8192, 26624], P(('col', 'rep'), 'row')
- new_second_scale: float32 [64, 208], P(('col', 'rep'), 'row')
The draws below stay inside these ranges and needn't reach their ends.
All inputs are finite; a program needn't handle non-finite values. Where the reference program divides by a largest or mean magnitude, that divisor is 1e-20 or more.
Results may differ from the reference program's by a relative error of at most 0.0095.
Values may be sent and summed in bfloat16 or wider, within the bound.
A program may use at most 192 MiB of HBM per device.

```python
import math
import jax
import jax.numpy as jnp
from jax import lax

D = 8192
FF = 26624
BLOCK = 128
REPLICAS = 2
TOK_REP = 2048
TOKENS = 4096


def steps_of(rng, extent, cuts, low, top_value):
    factor_of, own = 1.0, jax.random.fold_in(rng, 6)
    for position, blocks in cuts:
        steps = jnp.exp(jax.random.uniform(jax.random.fold_in(own, position), (blocks,), jnp.float32, low / len(cuts), top_value / len(cuts)))
        factor_of = factor_of * jnp.repeat(steps, extent[position] // blocks).reshape([-1 if axis == position else 1 for axis in range(len(extent))])
    return factor_of


def noise(rng, extent, deviation, most, split=(), kind=jnp.bfloat16):
    entries = deviation * jax.random.normal(rng, extent, jnp.float32)
    if split:
        entries = entries * steps_of(rng, extent, split, -0.22, 0.18)
    return jnp.clip(entries, -most, most).astype(kind)


def setup_inputs(seed: int = 0) -> dict:
    keys = jax.random.split(jax.random.key(seed), 9)
    return {
        "activations": noise(keys[0], (REPLICAS, TOK_REP, D), 1.0, 6.0, ((0, 2), (1, 16), (2, 4))),
        "out_grads": noise(keys[1], (REPLICAS, TOK_REP, FF), (TOKENS // 4) ** -0.5, 0.1875, ((0, 2), (1, 4), (2, 16))),
        "weight_code": jnp.clip(jax.random.uniform(keys[2], (D, FF), jnp.float32, -1.0, 1.0) * steps_of(keys[2], (D, FF), ((0, 8), (1, 16)), -0.4, 0.0), -1.0, 1.0).astype(jnp.bfloat16),
        "weight_scale": jnp.clip(jnp.exp(math.log(0.05) - 2.3025851 * jax.random.uniform(keys[3], (D // BLOCK, FF // BLOCK), jnp.float32) ** steps_of(keys[3], (D // BLOCK, FF // BLOCK), ((0, 8), (1, 16)), -0.2, 0.2)), 0.005, 0.05),
        "moment_code": jnp.clip(jax.random.uniform(keys[4], (D, FF), jnp.float32, -1.0, 1.0) * steps_of(keys[4], (D, FF), ((0, 8), (1, 16)), -0.4, 0.0), -1.0, 1.0).astype(jnp.bfloat16),
        "moment_scale": jnp.clip(jnp.exp(math.log(0.5) - 2.3025851 * jax.random.uniform(keys[5], (D // BLOCK, FF // BLOCK), jnp.float32) ** steps_of(keys[5], (D // BLOCK, FF // BLOCK), ((0, 8), (1, 16)), -0.2, 0.2)), 0.05, 0.5),
        "second_code": jnp.clip(0.049804688 + 0.9501953 * jax.random.uniform(keys[6], (D, FF), jnp.float32) ** steps_of(keys[6], (D, FF), ((0, 8), (1, 16)), -0.2, 0.2), 0.049804688, 1.0).astype(jnp.bfloat16),
        "second_scale": jnp.clip(jnp.exp(math.log(1.0) - 2.9957323 * jax.random.uniform(keys[7], (D // BLOCK, FF // BLOCK), jnp.float32) ** steps_of(keys[7], (D // BLOCK, FF // BLOCK), ((0, 8), (1, 16)), -0.2, 0.2)), 0.05, 1.0),
    }


def dequantize(codes, scales):
    rows, cols = codes.shape
    blocks = codes.astype(jnp.float32).reshape(rows // 128, 128, cols // 128, 128)
    return (blocks * scales[:, None, :, None]).reshape(rows, cols)

def quantize(values):
    rows, cols = values.shape
    blocks = values.reshape(rows // 128, 128, cols // 128, 128)
    scales = lax.optimization_barrier(jnp.max(jnp.abs(blocks), axis=(1, 3))) + 1e-06
    codes = (blocks / scales[:, None, :, None]).reshape(rows, cols).astype(jnp.bfloat16)
    return (codes, scales)

def adamw_step(gradient, weight_code, weight_scale, moment_code, moment_scale, second_code, second_scale):
    weight = dequantize(weight_code, weight_scale)
    moment = dequantize(moment_code, moment_scale)
    second = dequantize(second_code, second_scale)
    moment1 = 0.9 * moment + 0.1 * gradient
    second1 = 0.95 * second + 0.05 * gradient * gradient
    bias_one = 1.0 - 0.9 ** 10
    bias_two = 1.0 - 0.95 ** 10
    update = moment1 / bias_one / (jnp.sqrt(second1 / bias_two) + 1e-08) + 0.1 * weight
    weight1 = weight - 0.01 * update
    new_w, new_ws = quantize(weight1)
    new_m, new_ms = quantize(moment1)
    new_v, new_vs = quantize(second1)
    return (new_w, new_ws, new_m, new_ms, new_v, new_vs)

def reference(activations, out_grads, weight_code, weight_scale, moment_code, moment_scale, second_code, second_scale):
    inputs_f = activations.astype(jnp.float32)
    count = FF // 128

    def column_block(index):
        start = (index * 128).astype(jnp.int32)
        grads_f = lax.dynamic_slice_in_dim(out_grads, start, 128, 2).astype(jnp.float32)
        gradient = jnp.einsum('rtd,rtf->df', inputs_f, grads_f)
        sblock = index.astype(jnp.int32)
        return adamw_step(gradient, lax.dynamic_slice_in_dim(weight_code, start, 128, 1), lax.dynamic_slice_in_dim(weight_scale, sblock, 1, 1), lax.dynamic_slice_in_dim(moment_code, start, 128, 1), lax.dynamic_slice_in_dim(moment_scale, sblock, 1, 1), lax.dynamic_slice_in_dim(second_code, start, 128, 1), lax.dynamic_slice_in_dim(second_scale, sblock, 1, 1))
    results = lax.map(column_block, jnp.arange(count, dtype=jnp.int32))

    def join_codes(stack):
        return jnp.transpose(stack, (1, 0, 2)).reshape(D, FF)

    def join_scales(stack):
        return jnp.transpose(stack[:, :, 0], (1, 0))
    return (join_codes(results[0]), join_scales(results[1]), join_codes(results[2]), join_scales(results[3]), join_codes(results[4]), join_scales(results[5]))
```

```python
import jax
import jax.numpy as jnp
from jax import lax
from jax.experimental import pallas as pl
from jax.experimental.pallas import tpu as pltpu
from jax.sharding import PartitionSpec as P

MESH = pl.DeviceIdType.MESH
F32 = jnp.float32
BF16 = jnp.bfloat16
CHUNKS = 13
BIAS_ONE = 1.0 - 0.9**10
BIAS_TWO = 1.0 - 0.95**10


def kernel(
    acts, grads, w_scale, m_scale, v_scale, w_code, m_code, v_code,
    w_out, ws_out, m_out, ms_out, v_out, vs_out,
    A, T, G, W, M, V, acc, new, peak, inv, scales, peer_scales,
    in_sem, own_sem, y_send, y_recv, z_send, z_recv, zf_send, zf_recv, sib_send, sib_recv,
    s1_send, s1_recv, sx_send, sx_recv, s4_send, s4_recv,
    w_send, w_recv, sc_send, sc_recv, wl_sem, m_sem, v_sem,
):
    r, c, p = lax.axis_index("row"), lax.axis_index("col"), lax.axis_index("rep")
    yh, z, k = r // 8, (r // 2) % 4, r % 2
    q, yo = 1 - p, 1 - yh

    def at(yh_, z_, k_, c_, p_):
        return (yh_ * 8 + z_ * 2 + k_, c_, p_)

    partner = at(yh, z, k, c, q)
    other = at(yo, z, k, c, q)
    across = at(yo, z, k, c, p)
    sibling = at(yh, z, 1 - k, c, p)
    z_next, z_prev, z_far = (z + 1) % 4, (z + 3) % 4, (z + 2) % 4
    c_next, c_prev, c_far = (c + 1) % 4, (c + 3) % 4, (c + 2) % 4
    z_dev = (at(yh, z_next, k, c, p), at(yh, z_prev, k, c, p))
    x_dev = (at(yh, z, k, c_next, p), at(yh, z, k, c_prev, p))

    def remote(src, dst, send, recv, device):
        return pltpu.make_async_remote_copy(
            src_ref=src, dst_ref=dst, send_sem=send, recv_sem=recv,
            device_id=device, device_id_type=MESH,
        )

    def own_rows(part, c_):
        return pl.ds(pl.multiple_of(c_ * 1024 + part * 512, 512), 512)

    def cols(j):
        return pl.ds(pl.multiple_of(j * 128, 128), 128)

    def load_own(j):
        return pltpu.make_async_copy(grads.at[:, cols(j)], G.at[j, own_rows(p, c)], own_sem.at[j])

    def start_own(j, carry):
        load_own(j).start()
        return carry

    lax.fori_loop(0, CHUNKS, start_own, 0)
    loads = [
        pltpu.make_async_copy(w_code, W, in_sem.at[0]),
        pltpu.make_async_copy(m_code, M, in_sem.at[1]),
        pltpu.make_async_copy(v_code, V, in_sem.at[2]),
    ]
    for load in loads:
        load.start()

    barrier = pltpu.get_barrier_semaphore()
    for device in (partner, other, across, sibling) + z_dev + x_dev:
        pl.semaphore_signal(barrier, inc=1, device_id=device, device_id_type=MESH)

    def idx(yh_, z_, k_, p_):
        return (yh_ * 2 + z_ // 2) * 8 + p_ * 4 + (z_ % 2) * 2 + k_

    mine = idx(yh, z, k, p)
    for i in range(8):
        A[mine, i * 128:(i + 1) * 128, :] = acts[:, pl.ds(pl.multiple_of(p * 1024 + i * 128, 128), 128)].T
        T[i * 128:(i + 1) * 128, :] = acts[:, pl.ds(pl.multiple_of(q * 1024 + i * 128, 128), 128)].T

    pl.semaphore_wait(barrier, 8)

    piece_yh = (yh, yh, yo, yo)
    piece_p = (p, q, q, p)

    def piece(i, z_, k_):
        return A.at[idx(piece_yh[i], z_, k_, piece_p[i])]

    def y_copy(i):
        src = A.at[mine] if i == 3 else T
        return remote(src, A.at[mine], y_send.at[i], y_recv.at[i], (None, partner, other, across)[i])

    def y_landed(i):
        got = piece(i, z, k)
        return remote(got, got, y_send.at[i], y_recv.at[i], (None, partner, other, across)[i])

    def z_copy(i, d):
        return remote(piece(i, z, k), piece(i, z, k), z_send.at[d, i], z_recv.at[d, i], z_dev[d])

    def z_landed(i, d):
        got = piece(i, (z_prev, z_next)[d], k)
        return remote(got, got, z_send.at[d, i], z_recv.at[d, i], z_dev[d])

    def zf_copy(i):
        d = i // 2
        got = piece(i, (z_prev, z_next)[d], k)
        return remote(got, got, zf_send.at[i], zf_recv.at[i], z_dev[d])

    def zf_landed(i):
        got = piece(i, z_far, k)
        return remote(got, got, zf_send.at[i], zf_recv.at[i], z_dev[i // 2])

    hops = (z, z_prev, z_next, z_far)

    def sib_copy(i, h):
        got = piece(i, hops[h], k)
        return remote(got, got, sib_send.at[h, i], sib_recv.at[h, i], sibling)

    def sib_landed(i, h):
        got = piece(i, hops[h], 1 - k)
        return remote(got, got, sib_send.at[h, i], sib_recv.at[h, i], sibling)

    def s1_copy(j):
        rows = G.at[j, own_rows(p, c)]
        return remote(rows, rows, s1_send.at[j], s1_recv.at[j], partner)

    def s1_landed(j):
        rows = G.at[j, own_rows(q, c)]
        return remote(rows, rows, s1_send.at[j], s1_recv.at[j], partner)

    def sx_copy(j, part, d):
        rows = G.at[j, own_rows((p, q)[part], c)]
        return remote(rows, rows, sx_send.at[part, d, j], sx_recv.at[part, d, j], x_dev[d])

    def sx_landed(j, part, d):
        rows = G.at[j, own_rows((p, q)[part], (c_prev, c_next)[d])]
        return remote(rows, rows, sx_send.at[part, d, j], sx_recv.at[part, d, j], x_dev[d])

    def s4_copy(j, d):
        rows = G.at[j, own_rows((p, q)[d], (c_prev, c_next)[d])]
        return remote(rows, rows, s4_send.at[d, j], s4_recv.at[d, j], x_dev[d])

    def s4_landed(j, d):
        rows = G.at[j, own_rows((p, q)[d], c_far)]
        return remote(rows, rows, s4_send.at[d, j], s4_recv.at[d, j], x_dev[d])

    def send_own(j):
        sx_copy(j, 0, 0).start()
        sx_copy(j, 0, 1).start()

    def send_partner(j):
        s1_landed(j).wait_recv()
        sx_copy(j, 1, 0).start()
        sx_copy(j, 1, 1).start()

    def forward(j):
        sx_landed(j, 0, 0).wait_recv()
        s4_copy(j, 0).start()
        sx_landed(j, 1, 1).wait_recv()
        s4_copy(j, 1).start()

    def x_step(j):
        forward(j)

        @pl.when(j + 2 < CHUNKS)
        def _():
            send_own(j + 2)
            send_partner(j + 2)

    for i in (1, 2, 3):
        y_copy(i).start()
    z_copy(0, 0).start()
    z_copy(0, 1).start()
    sib_copy(0, 0).start()

    def wait_own(j, carry):
        load_own(j).wait()
        return carry

    lax.fori_loop(0, CHUNKS, wait_own, 0)

    def start_s1(j, carry):
        s1_copy(j).start()
        return carry

    lax.fori_loop(0, CHUNKS, start_s1, 0)
    send_own(0)
    send_own(1)

    for i in (1, 2, 3):
        y_landed(i).wait_recv()
        z_copy(i, 0).start()
        z_copy(i, 1).start()
        sib_copy(i, 0).start()
    send_partner(0)
    send_partner(1)

    for i in range(4):
        z_landed(i, 0).wait_recv()
        if i < 2:
            zf_copy(i).start()
        sib_copy(i, 1).start()
        z_landed(i, 1).wait_recv()
        if i >= 2:
            zf_copy(i).start()
        sib_copy(i, 2).start()
        x_step(i)
    for i in range(4):
        zf_landed(i).wait_recv()
        sib_copy(i, 3).start()
    x_step(4)
    for load in loads:
        load.wait()
    for h in range(4):
        for i in range(4):
            sib_landed(i, h).wait_recv()

    lane = lax.broadcasted_iota(jnp.int32, (24, 128), 1)

    def w_copy(j):
        here = pl.ds(pl.multiple_of(p * 1024, 1024), 1024)
        return remote(W.at[:, cols(j)], w_out.at[here, cols(j)], w_send.at[j], w_recv.at[j], partner)

    def w_landed(j):
        there = pl.ds(pl.multiple_of(q * 1024, 1024), 1024)
        return remote(W.at[:, cols(j)], w_out.at[there, cols(j)], w_send.at[j], w_recv.at[j], partner)

    def stores(j):
        here = pl.ds(pl.multiple_of(p * 1024, 1024), 1024)
        return (
            pltpu.make_async_copy(W.at[:, cols(j)], w_out.at[here, cols(j)], wl_sem.at[j]),
            pltpu.make_async_copy(M.at[:, cols(j)], m_out.at[:, cols(j)], m_sem.at[j]),
            pltpu.make_async_copy(V.at[:, cols(j)], v_out.at[:, cols(j)], v_sem.at[j]),
        )

    def chunk(j, carry):
        step = 4 + (2 * j) // 3

        @pl.when(jnp.logical_and(j > 0, step != 4 + (2 * (j - 1)) // 3))
        def _():
            x_step(step)

        sx_landed(j, 1, 0).wait_recv()
        sx_landed(j, 0, 1).wait_recv()
        s4_landed(j, 0).wait_recv()
        s4_landed(j, 1).wait_recv()
        left = jnp.concatenate([A[i] for i in range(32)], axis=1)
        acc[...] = jnp.dot(left, G[j], preferred_element_type=F32)

        def update(d, carry):
            rows = pl.ds(pl.multiple_of(d * 128, 128), 128)
            g = acc[rows, :]
            weight = W[rows, cols(j)].astype(F32) * w_scale[d, j]
            moment = M[rows, cols(j)].astype(F32) * m_scale[d, j]
            second = V[rows, cols(j)].astype(F32) * v_scale[d, j]
            moment1 = 0.9 * moment + 0.1 * g
            second1 = 0.95 * second + 0.05 * (g * g)
            u = second1 * (1.0 / BIAS_TWO)
            denom = u * lax.rsqrt(u) + 1e-08
            weight1 = weight - 0.01 * ((moment1 * (1.0 / BIAS_ONE)) / denom + 0.1 * weight)
            for n, value in enumerate((weight1, moment1, second1)):
                new[n, rows, :] = value
                peak[n * 8 + d] = jnp.max(jnp.abs(value).reshape(16, 8, 128), axis=0)
            return carry

        lax.fori_loop(0, 8, update, 0)
        scale = jnp.max(jnp.max(peak[...], axis=1), axis=1, keepdims=True) + 1e-06
        scale = jnp.broadcast_to(scale, (24, 128))
        scales[...] = jnp.where(lane == j, scale, scales[...])
        inv[...] = 1.0 / scale

        def encode(d, carry):
            rows = pl.ds(pl.multiple_of(d * 128, 128), 128)
            for n, out in enumerate((W, M, V)):
                out[rows, cols(j)] = (new[n, rows, :] * inv[pl.ds(n * 8 + d, 1), :]).astype(BF16)
            return carry

        lax.fori_loop(0, 8, encode, 0)
        w_copy(j).start()
        for store in stores(j):
            store.start()
        return carry

    scales[...] = jnp.zeros_like(scales)
    lax.fori_loop(0, CHUNKS, chunk, 0)

    sc_copy = remote(scales.at[0:8], peer_scales, sc_send.at[0], sc_recv.at[0], partner)
    sc_copy.start()
    ms_out[...] = scales[8:16, :CHUNKS]
    vs_out[...] = scales[16:24, :CHUNKS]
    ws_out[pl.ds(pl.multiple_of(p * 8, 8), 8), :] = scales[0:8, :CHUNKS]

    for i in (1, 2, 3):
        y_copy(i).wait_send()
    for i in range(4):
        z_copy(i, 0).wait_send()
        z_copy(i, 1).wait_send()
        zf_copy(i).wait_send()
        for h in range(4):
            sib_copy(i, h).wait_send()

    def drain(j, carry):
        s1_copy(j).wait_send()
        for d in range(2):
            sx_copy(j, 0, d).wait_send()
            sx_copy(j, 1, d).wait_send()
            s4_copy(j, d).wait_send()
        for store in stores(j):
            store.wait()
        w_copy(j).wait_send()
        w_landed(j).wait_recv()
        return carry

    lax.fori_loop(0, CHUNKS, drain, 0)
    sc_copy.wait()
    ws_out[pl.ds(pl.multiple_of(q * 8, 8), 8), :] = peer_scales[:, :CHUNKS]


def per_device(
    activations, out_grads, weight_code, weight_scale,
    moment_code, moment_scale, second_code, second_scale,
):
    vmem = pl.BlockSpec(memory_space=pltpu.VMEM)
    smem = pl.BlockSpec(memory_space=pltpu.SMEM)
    hbm = pl.BlockSpec(memory_space=pl.ANY)
    dma = pltpu.SemaphoreType.DMA
    shape = jax.ShapeDtypeStruct
    return pl.pallas_call(
        kernel,
        out_shape=(
            shape((2048, 1664), BF16), shape((16, 13), F32),
            shape((1024, 1664), BF16), shape((8, 13), F32),
            shape((1024, 1664), BF16), shape((8, 13), F32),
        ),
        in_specs=[vmem, hbm, smem, smem, smem, hbm, hbm, hbm],
        out_specs=(hbm, vmem, hbm, vmem, hbm, vmem),
        scratch_shapes=[
            pltpu.VMEM((32, 1024, 128), BF16),
            pltpu.VMEM((1024, 128), BF16),
            pltpu.VMEM((CHUNKS, 4096, 128), BF16),
            pltpu.VMEM((1024, 1664), BF16),
            pltpu.VMEM((1024, 1664), BF16),
            pltpu.VMEM((1024, 1664), BF16),
            pltpu.VMEM((1024, 128), F32),
            pltpu.VMEM((3, 1024, 128), F32),
            pltpu.VMEM((24, 8, 128), F32),
            pltpu.VMEM((24, 128), F32),
            pltpu.VMEM((24, 128), F32),
            pltpu.VMEM((8, 128), F32),
            dma((3,)), dma((CHUNKS,)),
            dma((4,)), dma((4,)),
            dma((2, 4)), dma((2, 4)),
            dma((4,)), dma((4,)),
            dma((4, 4)), dma((4, 4)),
            dma((CHUNKS,)), dma((CHUNKS,)),
            dma((2, 2, CHUNKS)), dma((2, 2, CHUNKS)),
            dma((2, CHUNKS)), dma((2, CHUNKS)),
            dma((CHUNKS,)), dma((CHUNKS,)),
            dma((1,)), dma((1,)),
            dma((CHUNKS,)), dma((CHUNKS,)), dma((CHUNKS,)),
        ],
        compiler_params=pltpu.CompilerParams(
            collective_id=0, has_side_effects=True, vmem_limit_bytes=56 << 20
        ),
        cost_estimate=pl.CostEstimate(
            flops=2 * 1024 * 1664 * 4096, bytes_accessed=26 << 20, transcendentals=2 * 1024 * 1664
        ),
    )(
        activations[0], out_grads[0], weight_scale, moment_scale, second_scale,
        weight_code, moment_code, second_code,
    )


def solution(mesh):
    return jax.shard_map(
        per_device,
        mesh=mesh,
        in_specs=(
            P("rep", "row", "col"),
            P("rep", "col", "row"),
            P(("col", "rep"), "row"),
            P(("col", "rep"), "row"),
            P(("col", "rep"), "row"),
            P(("col", "rep"), "row"),
            P(("col", "rep"), "row"),
            P(("col", "rep"), "row"),
        ),
        out_specs=(
            P("col", "row"),
            P("col", "row"),
            P(("col", "rep"), "row"),
            P(("col", "rep"), "row"),
            P(("col", "rep"), "row"),
            P(("col", "rep"), "row"),
        ),
        check_vma=False,
    )
```

```python
import functools

import jax
import jax.numpy as jnp
from jax import lax
from jax.experimental import pallas as pl
from jax.experimental.pallas import tpu as pltpu
from jax.sharding import PartitionSpec as P

MESH = pl.DeviceIdType.MESH
F32 = jnp.float32
BF16 = jnp.bfloat16
CHUNKS = 13
BIAS_ONE = 1.0 - 0.9**10
BIAS_TWO = 1.0 - 0.95**10


def kernel(
    acts_in, grads, w_scale, m_scale, v_scale, w_code, m_code, v_code,
    W, peer_w, M, V, scales,
    acts, A, T, G, acc, new, peak, inv,
    in_sem, own_sem, y_send, y_recv, z_send, z_recv, zf_send, zf_recv, sib_send, sib_recv,
    s1_send, s1_recv, sx_send, sx_recv, s4_send, s4_recv,
    w_send, w_recv, sc_send, sc_recv,
):
    r, c, p = lax.axis_index("row"), lax.axis_index("col"), lax.axis_index("rep")
    yh, z, k = r // 8, (r // 2) % 4, r % 2
    q, yo = 1 - p, 1 - yh

    def at(yh_, z_, k_, c_, p_):
        return (yh_ * 8 + z_ * 2 + k_, c_, p_)

    partner = at(yh, z, k, c, q)
    other = at(yo, z, k, c, q)
    across = at(yo, z, k, c, p)
    sibling = at(yh, z, 1 - k, c, p)
    z_next, z_prev, z_far = (z + 1) % 4, (z + 3) % 4, (z + 2) % 4
    c_next, c_prev, c_far = (c + 1) % 4, (c + 3) % 4, (c + 2) % 4
    z_dev = (at(yh, z_next, k, c, p), at(yh, z_prev, k, c, p))
    x_dev = (at(yh, z, k, c_next, p), at(yh, z, k, c_prev, p))

    def remote(src, dst, send, recv, device):
        return pltpu.make_async_remote_copy(
            src_ref=src, dst_ref=dst, send_sem=send, recv_sem=recv,
            device_id=device, device_id_type=MESH,
        )

    def own_rows(part, c_):
        return pl.ds(pl.multiple_of(c_ * 1024 + part * 512, 512), 512)

    def cols(j):
        return pl.ds(pl.multiple_of(j * 128, 128), 128)

    def load_own(j):
        return pltpu.make_async_copy(grads.at[:, cols(j)], G.at[j, own_rows(p, c)], own_sem.at[j])

    def start_own(j, carry):
        load_own(j).start()
        return carry

    lax.fori_loop(0, CHUNKS, start_own, 0)
    loads = [
        pltpu.make_async_copy(w_code, W, in_sem.at[0]),
        pltpu.make_async_copy(m_code, M, in_sem.at[1]),
        pltpu.make_async_copy(v_code, V, in_sem.at[2]),
    ]
    load_acts = pltpu.make_async_copy(acts_in, acts, in_sem.at[3])
    load_acts.start()

    barrier = pltpu.get_barrier_semaphore()
    for device in (partner, other, across, sibling) + z_dev + x_dev:
        pl.semaphore_signal(barrier, inc=1, device_id=device, device_id_type=MESH)

    scales[0:24, :] = jnp.zeros((24, 128), F32)
    load_acts.wait()

    def idx(yh_, z_, k_, p_):
        return (yh_ * 2 + z_ // 2) * 8 + p_ * 4 + (z_ % 2) * 2 + k_

    mine = idx(yh, z, k, p)
    for i in range(8):
        A[mine, i * 128:(i + 1) * 128, :] = acts[:, pl.ds(pl.multiple_of(p * 1024 + i * 128, 128), 128)].T
        T[i * 128:(i + 1) * 128, :] = acts[:, pl.ds(pl.multiple_of(q * 1024 + i * 128, 128), 128)].T

    pl.semaphore_wait(barrier, 8)

    piece_yh = (yh, yh, yo, yo)
    piece_p = (p, q, q, p)

    def piece(i, z_, k_):
        return A.at[idx(piece_yh[i], z_, k_, piece_p[i])]

    def y_copy(i):
        src = A.at[mine] if i == 3 else T
        return remote(src, A.at[mine], y_send.at[i], y_recv.at[i], (None, partner, other, across)[i])

    def y_landed(i):
        got = piece(i, z, k)
        return remote(got, got, y_send.at[i], y_recv.at[i], (None, partner, other, across)[i])

    def z_copy(i, d):
        return remote(piece(i, z, k), piece(i, z, k), z_send.at[d, i], z_recv.at[d, i], z_dev[d])

    def z_landed(i, d):
        got = piece(i, (z_prev, z_next)[d], k)
        return remote(got, got, z_send.at[d, i], z_recv.at[d, i], z_dev[d])

    def zf_copy(i):
        d = i // 2
        got = piece(i, (z_prev, z_next)[d], k)
        return remote(got, got, zf_send.at[i], zf_recv.at[i], z_dev[d])

    def zf_landed(i):
        got = piece(i, z_far, k)
        return remote(got, got, zf_send.at[i], zf_recv.at[i], z_dev[i // 2])

    hops = (z, z_prev, z_next, z_far)

    def sib_copy(i, h):
        got = piece(i, hops[h], k)
        return remote(got, got, sib_send.at[h, i], sib_recv.at[h, i], sibling)

    def sib_landed(i, h):
        got = piece(i, hops[h], 1 - k)
        return remote(got, got, sib_send.at[h, i], sib_recv.at[h, i], sibling)

    def s1_copy(j):
        rows = G.at[j, own_rows(p, c)]
        return remote(rows, rows, s1_send.at[j], s1_recv.at[j], partner)

    def s1_landed(j):
        rows = G.at[j, own_rows(q, c)]
        return remote(rows, rows, s1_send.at[j], s1_recv.at[j], partner)

    def sx_copy(j, part, d):
        rows = G.at[j, own_rows((p, q)[part], c)]
        return remote(rows, rows, sx_send.at[part, d, j], sx_recv.at[part, d, j], x_dev[d])

    def sx_landed(j, part, d):
        rows = G.at[j, own_rows((p, q)[part], (c_prev, c_next)[d])]
        return remote(rows, rows, sx_send.at[part, d, j], sx_recv.at[part, d, j], x_dev[d])

    def s4_copy(j, d):
        rows = G.at[j, own_rows((p, q)[d], (c_prev, c_next)[d])]
        return remote(rows, rows, s4_send.at[d, j], s4_recv.at[d, j], x_dev[d])

    def s4_landed(j, d):
        rows = G.at[j, own_rows((p, q)[d], c_far)]
        return remote(rows, rows, s4_send.at[d, j], s4_recv.at[d, j], x_dev[d])

    def send_own(j):
        sx_copy(j, 0, 0).start()
        sx_copy(j, 0, 1).start()

    def send_partner(j):
        s1_landed(j).wait_recv()
        sx_copy(j, 1, 0).start()
        sx_copy(j, 1, 1).start()

    def forward(j):
        sx_landed(j, 0, 0).wait_recv()
        s4_copy(j, 0).start()
        sx_landed(j, 1, 1).wait_recv()
        s4_copy(j, 1).start()

    def x_step(j):
        forward(j)

        @pl.when(j < 3)
        def _():
            send_partner(j + 3)

        @pl.when(jnp.logical_and(j > 3, j < CHUNKS - 2))
        def _():
            send_partner(j + 2)
            send_own(j + 2)

    def relay(i):
        z_landed(i, 0).wait_recv()
        if i < 2:
            zf_copy(i).start()
        sib_copy(i, 1).start()
        z_landed(i, 1).wait_recv()
        if i >= 2:
            zf_copy(i).start()
        sib_copy(i, 2).start()

    def spread(i):
        y_landed(i).wait_recv()
        z_copy(i, 0).start()
        z_copy(i, 1).start()
        sib_copy(i, 0).start()

    def finish(i):
        zf_landed(i).wait_recv()
        sib_copy(i, 3).start()

    for i in (1, 2, 3):
        y_copy(i).start()
    z_copy(0, 0).start()
    z_copy(0, 1).start()

    def wait_own(j, carry):
        load_own(j).wait()
        return carry

    lax.fori_loop(0, CHUNKS, wait_own, 0)

    def start_own_sends(j, carry):
        send_own(j)
        return carry

    lax.fori_loop(0, 6, start_own_sends, 0)

    def start_s1(j, carry):
        s1_copy(j).start()
        return carry

    lax.fori_loop(0, CHUNKS, start_s1, 0)
    sib_copy(0, 0).start()
    for load in loads:
        load.start()

    spread(1)
    spread(2)
    relay(0)
    spread(3)
    relay(1)
    send_partner(0)
    send_partner(1)
    relay(2)
    send_partner(2)
    x_step(0)
    x_step(1)
    x_step(2)
    relay(3)
    finish(0)
    finish(2)
    x_step(3)
    finish(1)
    finish(3)
    x_step(4)
    for load in loads:
        load.wait()
    for h in range(4):
        for i in range(4):
            sib_landed(i, h).wait_recv()

    lane = lax.broadcasted_iota(jnp.int32, (24, 128), 1)

    def w_copy(j):
        return remote(W.at[:, cols(j)], peer_w.at[:, cols(j)], w_send.at[j], w_recv.at[j], partner)

    def chunk(j, carry):
        @pl.when(j == 3)
        def _():
            x_step(5)

        @pl.when(jnp.logical_and(j > 4, j < CHUNKS - 1))
        def _():
            x_step(j + 1)

        sx_landed(j, 1, 0).wait_recv()
        sx_landed(j, 0, 1).wait_recv()
        s4_landed(j, 0).wait_recv()
        s4_landed(j, 1).wait_recv()
        left = jnp.concatenate([A[i] for i in range(32)], axis=1)
        acc[...] = jnp.dot(left, G[j], preferred_element_type=F32)

        def update(d, carry):
            rows = pl.ds(pl.multiple_of(d * 128, 128), 128)
            g = acc[rows, :]
            weight = W[rows, cols(j)].astype(F32) * w_scale[d, j]
            moment = M[rows, cols(j)].astype(F32) * m_scale[d, j]
            second = V[rows, cols(j)].astype(F32) * v_scale[d, j]
            moment1 = 0.9 * moment + 0.1 * g
            second1 = 0.95 * second + 0.05 * (g * g)
            u = second1 * (1.0 / BIAS_TWO)
            denom = u * lax.rsqrt(u) + 1e-08
            weight1 = weight - 0.01 * ((moment1 * (1.0 / BIAS_ONE)) / denom + 0.1 * weight)
            for n, value in enumerate((weight1, moment1, second1)):
                new[n, rows, :] = value
                peak[n * 8 + d] = jnp.max(jnp.abs(value).reshape(16, 8, 128), axis=0)
            return carry

        lax.fori_loop(0, 8, update, 0)
        scale = jnp.max(jnp.max(peak[...], axis=1), axis=1, keepdims=True) + 1e-06
        scale = jnp.broadcast_to(scale, (24, 128))
        scales[0:24, :] = jnp.where(lane == j, scale, scales[0:24, :])
        inv[...] = 1.0 / scale

        def encode(d, carry):
            rows = pl.ds(pl.multiple_of(d * 128, 128), 128)
            for n, out in enumerate((W, M, V)):
                out[rows, cols(j)] = (new[n, rows, :] * inv[pl.ds(n * 8 + d, 1), :]).astype(BF16)
            return carry

        lax.fori_loop(0, 8, encode, 0)
        w_copy(j).start()
        return carry

    lax.fori_loop(0, CHUNKS, chunk, 0)

    sc_copy = remote(scales.at[0:8], scales.at[24:32], sc_send.at[0], sc_recv.at[0], partner)
    sc_copy.start()

    for i in (1, 2, 3):
        y_copy(i).wait_send()
    for i in range(4):
        z_copy(i, 0).wait_send()
        z_copy(i, 1).wait_send()
        zf_copy(i).wait_send()
        for h in range(4):
            sib_copy(i, h).wait_send()

    def drain(j, carry):
        s1_copy(j).wait_send()
        for d in range(2):
            sx_copy(j, 0, d).wait_send()
            sx_copy(j, 1, d).wait_send()
            s4_copy(j, d).wait_send()
        w_copy(j).wait()
        return carry

    lax.fori_loop(0, CHUNKS, drain, 0)
    sc_copy.wait()


def store_kernel(W, peer_w, M, V, scales, w_out, ws_out, m_out, ms_out, v_out, vs_out, sem):
    p = lax.axis_index("rep")
    q = 1 - p
    copies = []
    for n in range(4):
        rows = pl.ds(n * 256, 256)
        here = pl.ds(pl.multiple_of(p * 1024 + n * 256, 256), 256)
        there = pl.ds(pl.multiple_of(q * 1024 + n * 256, 256), 256)
        copies += [
            pltpu.make_async_copy(W.at[rows], w_out.at[here], sem.at[0, n]),
            pltpu.make_async_copy(peer_w.at[rows], w_out.at[there], sem.at[1, n]),
            pltpu.make_async_copy(M.at[rows], m_out.at[rows], sem.at[2, n]),
            pltpu.make_async_copy(V.at[rows], v_out.at[rows], sem.at[3, n]),
        ]
    for copy in copies:
        copy.start()
    ws_out[pl.ds(pl.multiple_of(p * 8, 8), 8), :] = scales[0:8, :CHUNKS]
    ws_out[pl.ds(pl.multiple_of(q * 8, 8), 8), :] = scales[24:32, :CHUNKS]
    ms_out[...] = scales[8:16, :CHUNKS]
    vs_out[...] = scales[16:24, :CHUNKS]
    for copy in copies:
        copy.wait()


def per_device(
    activations, out_grads, weight_code, weight_scale,
    moment_code, moment_scale, second_code, second_scale,
):
    vmem = pl.BlockSpec(memory_space=pltpu.VMEM)
    smem = pl.BlockSpec(memory_space=pltpu.SMEM)
    hbm = pl.BlockSpec(memory_space=pl.ANY)
    dma = pltpu.SemaphoreType.DMA
    shape = jax.ShapeDtypeStruct
    pinned = functools.partial(pltpu.with_memory_space_constraint, memory_space=pltpu.HBM)
    codes = pltpu.VMEM((1024, 1664), BF16)
    held = pl.pallas_call(
        kernel,
        out_shape=(codes, codes, codes, codes, pltpu.VMEM((32, 128), F32)),
        in_specs=[hbm, hbm, smem, smem, smem, hbm, hbm, hbm],
        out_specs=(vmem,) * 5,
        scratch_shapes=[
            pltpu.VMEM((128, 2048), BF16),
            pltpu.VMEM((32, 1024, 128), BF16),
            pltpu.VMEM((1024, 128), BF16),
            pltpu.VMEM((CHUNKS, 4096, 128), BF16),
            pltpu.VMEM((1024, 128), F32),
            pltpu.VMEM((3, 1024, 128), F32),
            pltpu.VMEM((24, 8, 128), F32),
            pltpu.VMEM((24, 128), F32),
            dma((4,)), dma((CHUNKS,)),
            dma((4,)), dma((4,)),
            dma((2, 4)), dma((2, 4)),
            dma((4,)), dma((4,)),
            dma((4, 4)), dma((4, 4)),
            dma((CHUNKS,)), dma((CHUNKS,)),
            dma((2, 2, CHUNKS)), dma((2, 2, CHUNKS)),
            dma((2, CHUNKS)), dma((2, CHUNKS)),
            dma((CHUNKS,)), dma((CHUNKS,)),
            dma((1,)), dma((1,)),
        ],
        compiler_params=pltpu.CompilerParams(
            collective_id=0, has_side_effects=True, vmem_limit_bytes=32 << 20
        ),
        cost_estimate=pl.CostEstimate(
            flops=2 * 1024 * 1664 * 4096, bytes_accessed=26 << 20, transcendentals=2 * 1024 * 1664
        ),
    )(
        pinned(activations[0]), pinned(out_grads[0]),
        pinned(weight_scale), pinned(moment_scale), pinned(second_scale),
        pinned(weight_code), pinned(moment_code), pinned(second_code),
    )
    return pl.pallas_call(
        store_kernel,
        out_shape=(
            shape((2048, 1664), BF16), shape((16, 13), F32),
            shape((1024, 1664), BF16), shape((8, 13), F32),
            shape((1024, 1664), BF16), shape((8, 13), F32),
        ),
        in_specs=[vmem] * 5,
        out_specs=(hbm, vmem, hbm, vmem, hbm, vmem),
        scratch_shapes=[dma((4, 4))],
        compiler_params=pltpu.CompilerParams(vmem_limit_bytes=8 << 20),
        cost_estimate=pl.CostEstimate(flops=0, bytes_accessed=26 << 20, transcendentals=0),
    )(*(pltpu.with_memory_space_constraint(x, pltpu.VMEM) for x in held))


def solution(mesh):
    return jax.shard_map(
        per_device,
        mesh=mesh,
        in_specs=(
            P("rep", "row", "col"),
            P("rep", "col", "row"),
            P(("col", "rep"), "row"),
            P(("col", "rep"), "row"),
            P(("col", "rep"), "row"),
            P(("col", "rep"), "row"),
            P(("col", "rep"), "row"),
            P(("col", "rep"), "row"),
        ),
        out_specs=(
            P("col", "row"),
            P("col", "row"),
            P(("col", "rep"), "row"),
            P(("col", "rep"), "row"),
            P(("col", "rep"), "row"),
            P(("col", "rep"), "row"),
        ),
        check_vma=False,
    )
```

```python
import functools

import jax
import jax.numpy as jnp
from jax import lax
from jax.experimental import pallas as pl
from jax.experimental.pallas import tpu as pltpu
from jax.sharding import PartitionSpec as P

MESH = pl.DeviceIdType.MESH
F32 = jnp.float32
BF16 = jnp.bfloat16
CHUNKS = 13
BIAS_ONE = 1.0 - 0.9**10
BIAS_TWO = 1.0 - 0.95**10


def kernel(
    acts_in, grads, w_scale_in, m_scale_in, v_scale_in, w_code, m_code, v_code,
    W, peer_w, M, V, scales,
    acts, A, T, G, acc, new, peak, inv, w_scale, m_scale, v_scale,
    in_sem, own_sem, y_send, y_recv, z_send, z_recv, zf_send, zf_recv, sib_send, sib_recv,
    s1_send, s1_recv, sx_send, sx_recv, s4_send, s4_recv,
    w_send, w_recv, sc_send, sc_recv,
):
    r, c, p = lax.axis_index("row"), lax.axis_index("col"), lax.axis_index("rep")
    yh, z, k = r // 8, (r // 2) % 4, r % 2
    q, yo = 1 - p, 1 - yh

    def at(yh_, z_, k_, c_, p_):
        return (yh_ * 8 + z_ * 2 + k_, c_, p_)

    partner = at(yh, z, k, c, q)
    other = at(yo, z, k, c, q)
    across = at(yo, z, k, c, p)
    sibling = at(yh, z, 1 - k, c, p)
    z_next, z_prev, z_far = (z + 1) % 4, (z + 3) % 4, (z + 2) % 4
    c_next, c_prev, c_far = (c + 1) % 4, (c + 3) % 4, (c + 2) % 4
    z_dev = (at(yh, z_next, k, c, p), at(yh, z_prev, k, c, p))
    x_dev = (at(yh, z, k, c_next, p), at(yh, z, k, c_prev, p))

    barrier = pltpu.get_barrier_semaphore()
    for device in (partner, other, across, sibling) + z_dev + x_dev:
        pl.semaphore_signal(barrier, inc=1, device_id=device, device_id_type=MESH)

    def remote(src, dst, send, recv, device):
        return pltpu.make_async_remote_copy(
            src_ref=src, dst_ref=dst, send_sem=send, recv_sem=recv,
            device_id=device, device_id_type=MESH,
        )

    def own_rows(part, c_):
        return pl.ds(pl.multiple_of(c_ * 1024 + part * 512, 512), 512)

    def cols(j):
        return pl.ds(pl.multiple_of(j * 128, 128), 128)

    def load_own(j):
        return pltpu.make_async_copy(grads.at[:, cols(j)], G.at[j, own_rows(p, c)], own_sem.at[j])

    def start_own(j, carry):
        load_own(j).start()
        return carry

    lax.fori_loop(0, CHUNKS, start_own, 0)
    loads = [
        pltpu.make_async_copy(w_code, W, in_sem.at[0]),
        pltpu.make_async_copy(m_code, M, in_sem.at[1]),
        pltpu.make_async_copy(v_code, V, in_sem.at[2]),
        pltpu.make_async_copy(w_scale_in, w_scale, in_sem.at[4]),
        pltpu.make_async_copy(m_scale_in, m_scale, in_sem.at[5]),
        pltpu.make_async_copy(v_scale_in, v_scale, in_sem.at[6]),
    ]
    load_acts = pltpu.make_async_copy(acts_in, acts, in_sem.at[3])
    load_acts.start()

    scales[0:24, :] = jnp.zeros((24, 128), F32)
    load_acts.wait()

    def idx(yh_, z_, k_, p_):
        return (yh_ * 2 + z_ // 2) * 8 + p_ * 4 + (z_ % 2) * 2 + k_

    mine = idx(yh, z, k, p)
    for i in range(8):
        A[mine, i * 128:(i + 1) * 128, :] = acts[:, pl.ds(pl.multiple_of(p * 1024 + i * 128, 128), 128)].T
        T[i * 128:(i + 1) * 128, :] = acts[:, pl.ds(pl.multiple_of(q * 1024 + i * 128, 128), 128)].T

    pl.semaphore_wait(barrier, 8)

    piece_yh = (yh, yh, yo, yo)
    piece_p = (p, q, q, p)

    def piece(i, z_, k_):
        return A.at[idx(piece_yh[i], z_, k_, piece_p[i])]

    def y_copy(i):
        src = A.at[mine] if i == 3 else T
        return remote(src, A.at[mine], y_send.at[i], y_recv.at[i], (None, partner, other, across)[i])

    def y_landed(i):
        got = piece(i, z, k)
        return remote(got, got, y_send.at[i], y_recv.at[i], (None, partner, other, across)[i])

    def z_copy(i, d):
        return remote(piece(i, z, k), piece(i, z, k), z_send.at[d, i], z_recv.at[d, i], z_dev[d])

    def z_landed(i, d):
        got = piece(i, (z_prev, z_next)[d], k)
        return remote(got, got, z_send.at[d, i], z_recv.at[d, i], z_dev[d])

    def zf_copy(i):
        d = i // 2
        got = piece(i, (z_prev, z_next)[d], k)
        return remote(got, got, zf_send.at[i], zf_recv.at[i], z_dev[d])

    def zf_landed(i):
        got = piece(i, z_far, k)
        return remote(got, got, zf_send.at[i], zf_recv.at[i], z_dev[i // 2])

    hops = (z, z_prev, z_next, z_far)

    def sib_copy(i, h):
        got = piece(i, hops[h], k)
        return remote(got, got, sib_send.at[h, i], sib_recv.at[h, i], sibling)

    def sib_landed(i, h):
        got = piece(i, hops[h], 1 - k)
        return remote(got, got, sib_send.at[h, i], sib_recv.at[h, i], sibling)

    def s1_copy(j):
        rows = G.at[j, own_rows(p, c)]
        return remote(rows, rows, s1_send.at[j], s1_recv.at[j], partner)

    def s1_landed(j):
        rows = G.at[j, own_rows(q, c)]
        return remote(rows, rows, s1_send.at[j], s1_recv.at[j], partner)

    def sx_copy(j, part, d):
        rows = G.at[j, own_rows((p, q)[part], c)]
        return remote(rows, rows, sx_send.at[part, d, j], sx_recv.at[part, d, j], x_dev[d])

    def sx_landed(j, part, d):
        rows = G.at[j, own_rows((p, q)[part], (c_prev, c_next)[d])]
        return remote(rows, rows, sx_send.at[part, d, j], sx_recv.at[part, d, j], x_dev[d])

    def s4_copy(j, d):
        rows = G.at[j, own_rows((p, q)[d], (c_prev, c_next)[d])]
        return remote(rows, rows, s4_send.at[d, j], s4_recv.at[d, j], x_dev[d])

    def s4_landed(j, d):
        rows = G.at[j, own_rows((p, q)[d], c_far)]
        return remote(rows, rows, s4_send.at[d, j], s4_recv.at[d, j], x_dev[d])

    def send_own(j):
        sx_copy(j, 0, 0).start()
        sx_copy(j, 0, 1).start()

    def send_partner(j):
        s1_landed(j).wait_recv()
        sx_copy(j, 1, 0).start()
        sx_copy(j, 1, 1).start()

    def forward(j):
        sx_landed(j, 0, 0).wait_recv()
        s4_copy(j, 0).start()
        sx_landed(j, 1, 1).wait_recv()
        s4_copy(j, 1).start()

    def x_step(j):
        forward(j)

        @pl.when(j < CHUNKS - 4)
        def _():
            send_partner(j + 3)

        @pl.when(jnp.logical_and(j > 2, j < CHUNKS - 4))
        def _():
            send_own(j + 3)

        @pl.when(j == CHUNKS - 3)
        def _():
            send_partner(j + 2)
            send_own(j + 2)

    def relay(i):
        z_landed(i, 0).wait_recv()
        if i < 2:
            zf_copy(i).start()
        sib_copy(i, 1).start()
        z_landed(i, 1).wait_recv()
        if i >= 2:
            zf_copy(i).start()
        sib_copy(i, 2).start()

    def spread(i):
        y_landed(i).wait_recv()
        z_copy(i, 0).start()
        z_copy(i, 1).start()
        sib_copy(i, 0).start()

    def finish(i):
        zf_landed(i).wait_recv()
        sib_copy(i, 3).start()

    for i in (1, 2, 3):
        y_copy(i).start()
    z_copy(0, 0).start()
    z_copy(0, 1).start()

    def wait_own(j, carry):
        load_own(j).wait()
        return carry

    lax.fori_loop(0, CHUNKS, wait_own, 0)

    def start_own_sends(j, carry):
        send_own(j)
        return carry

    lax.fori_loop(0, 6, start_own_sends, 0)

    def start_s1(j, carry):
        s1_copy(j).start()
        return carry

    lax.fori_loop(0, CHUNKS, start_s1, 0)
    sib_copy(0, 0).start()
    for load in loads:
        load.start()

    spread(1)
    spread(2)
    relay(0)
    spread(3)
    relay(1)
    send_partner(0)
    send_partner(1)
    relay(2)
    send_partner(2)
    x_step(0)
    x_step(1)
    x_step(2)
    relay(3)
    finish(0)
    finish(2)
    x_step(3)
    x_step(4)
    finish(1)
    finish(3)
    for load in loads:
        load.wait()
    for h in range(4):
        for i in range(4):
            sib_landed(i, h).wait_recv()

    lane = lax.broadcasted_iota(jnp.int32, (24, 128), 1)

    def w_copy(j):
        return remote(W.at[:, cols(j)], peer_w.at[:, cols(j)], w_send.at[j], w_recv.at[j], partner)

    sc_copy = remote(scales.at[0:8], scales.at[24:32], sc_send.at[0], sc_recv.at[0], partner)

    def product(j, c_):
        left = jnp.concatenate([A[c_ * 8 + i] for i in range(8)], axis=1)
        right = G[j, pl.ds(pl.multiple_of(c_ * 1024, 1024), 1024), :]
        return jnp.dot(left, right, preferred_element_type=F32)

    def chunk(j, carry):
        @pl.when(jnp.logical_or(j == 1, j == 3))
        def _():
            x_step(5 + j // 2)

        @pl.when(jnp.logical_or(j == 5, jnp.logical_and(j > 6, j < CHUNKS - 1)))
        def _():
            x_step(jnp.where(j == 5, 7, j + 1))

        sx_landed(j, 1, 0).wait_recv()
        sx_landed(j, 0, 1).wait_recv()
        acc[...] = product(j, c) + product(j, c_prev) + product(j, c_next)
        s4_landed(j, 0).wait_recv()
        s4_landed(j, 1).wait_recv()
        acc[...] += product(j, c_far)

        def update(d, carry):
            rows = pl.ds(pl.multiple_of(d * 128, 128), 128)
            g = acc[rows, :]
            weight = W[rows, cols(j)].astype(F32) * w_scale[d, j]
            moment = M[rows, cols(j)].astype(F32) * m_scale[d, j]
            second = V[rows, cols(j)].astype(F32) * v_scale[d, j]
            moment1 = 0.9 * moment + 0.1 * g
            second1 = 0.95 * second + 0.05 * (g * g)
            u = second1 * (1.0 / BIAS_TWO)
            denom = u * lax.rsqrt(u) + 1e-08
            weight1 = weight - 0.01 * ((moment1 * (1.0 / BIAS_ONE)) / denom + 0.1 * weight)
            for n, value in enumerate((weight1, moment1, second1)):
                new[n, rows, :] = value
                peak[n * 8 + d] = jnp.max(jnp.abs(value).reshape(16, 8, 128), axis=0)
            return carry

        lax.fori_loop(0, 8, update, 0)
        scale = jnp.max(jnp.max(peak[...], axis=1), axis=1, keepdims=True) + 1e-06
        scale = jnp.broadcast_to(scale, (24, 128))
        scales[0:24, :] = jnp.where(lane == j, scale, scales[0:24, :])
        inv[...] = 1.0 / scale

        @pl.when(j == CHUNKS - 1)
        def _():
            sc_copy.start()

        def encode(d, carry):
            rows = pl.ds(pl.multiple_of(d * 128, 128), 128)
            for n, out in enumerate((W, M, V)):
                out[rows, cols(j)] = (new[n, rows, :] * inv[pl.ds(n * 8 + d, 1), :]).astype(BF16)
            return carry

        lax.fori_loop(0, 8, encode, 0)
        w_copy(j).start()
        return carry

    lax.fori_loop(0, CHUNKS, chunk, 0)

    for i in (1, 2, 3):
        y_copy(i).wait_send()
    for i in range(4):
        z_copy(i, 0).wait_send()
        z_copy(i, 1).wait_send()
        zf_copy(i).wait_send()
        for h in range(4):
            sib_copy(i, h).wait_send()

    def drain(j, carry):
        s1_copy(j).wait_send()
        for d in range(2):
            sx_copy(j, 0, d).wait_send()
            sx_copy(j, 1, d).wait_send()
            s4_copy(j, d).wait_send()
        w_copy(j).wait()
        return carry

    lax.fori_loop(0, CHUNKS, drain, 0)
    sc_copy.wait()


def store_kernel(W, peer_w, M, V, scales, w_out, ws_out, m_out, ms_out, v_out, vs_out, ws, ms, vs, sem, sc_sem):
    p = lax.axis_index("rep")
    q = 1 - p
    copies = []
    for n in range(4):
        rows = pl.ds(n * 256, 256)
        here = pl.ds(pl.multiple_of(p * 1024 + n * 256, 256), 256)
        there = pl.ds(pl.multiple_of(q * 1024 + n * 256, 256), 256)
        copies += [
            pltpu.make_async_copy(W.at[rows], w_out.at[here], sem.at[0, n]),
            pltpu.make_async_copy(peer_w.at[rows], w_out.at[there], sem.at[1, n]),
            pltpu.make_async_copy(M.at[rows], m_out.at[rows], sem.at[2, n]),
            pltpu.make_async_copy(V.at[rows], v_out.at[rows], sem.at[3, n]),
        ]
    for copy in copies:
        copy.start()
    ws[pl.ds(pl.multiple_of(p * 8, 8), 8), :] = scales[0:8, :CHUNKS]
    ws[pl.ds(pl.multiple_of(q * 8, 8), 8), :] = scales[24:32, :CHUNKS]
    ms[...] = scales[8:16, :CHUNKS]
    vs[...] = scales[16:24, :CHUNKS]
    for n, (src, dst) in enumerate(((ws, ws_out), (ms, ms_out), (vs, vs_out))):
        copies.append(pltpu.make_async_copy(src, dst, sc_sem.at[n]))
        copies[-1].start()
    for copy in copies:
        copy.wait()


def per_device(
    activations, out_grads, weight_code, weight_scale,
    moment_code, moment_scale, second_code, second_scale,
):
    vmem = pl.BlockSpec(memory_space=pltpu.VMEM)
    hbm = pl.BlockSpec(memory_space=pl.ANY)
    dma = pltpu.SemaphoreType.DMA
    shape = jax.ShapeDtypeStruct
    pinned = functools.partial(pltpu.with_memory_space_constraint, memory_space=pltpu.HBM)
    codes = pltpu.VMEM((1024, 1664), BF16)
    held = pl.pallas_call(
        kernel,
        out_shape=(codes, codes, codes, codes, pltpu.VMEM((32, 128), F32)),
        in_specs=[hbm] * 8,
        out_specs=(vmem,) * 5,
        scratch_shapes=[
            pltpu.VMEM((128, 2048), BF16),
            pltpu.VMEM((32, 1024, 128), BF16),
            pltpu.VMEM((1024, 128), BF16),
            pltpu.VMEM((CHUNKS, 4096, 128), BF16),
            pltpu.VMEM((1024, 128), F32),
            pltpu.VMEM((3, 1024, 128), F32),
            pltpu.VMEM((24, 8, 128), F32),
            pltpu.VMEM((24, 128), F32),
            pltpu.SMEM((8, 13), F32),
            pltpu.SMEM((8, 13), F32),
            pltpu.SMEM((8, 13), F32),
            dma((7,)), dma((CHUNKS,)),
            dma((4,)), dma((4,)),
            dma((2, 4)), dma((2, 4)),
            dma((4,)), dma((4,)),
            dma((4, 4)), dma((4, 4)),
            dma((CHUNKS,)), dma((CHUNKS,)),
            dma((2, 2, CHUNKS)), dma((2, 2, CHUNKS)),
            dma((2, CHUNKS)), dma((2, CHUNKS)),
            dma((CHUNKS,)), dma((CHUNKS,)),
            dma((1,)), dma((1,)),
        ],
        compiler_params=pltpu.CompilerParams(
            collective_id=0, has_side_effects=True, vmem_limit_bytes=32 << 20
        ),
        cost_estimate=pl.CostEstimate(
            flops=2 * 1024 * 1664 * 4096, bytes_accessed=26 << 20, transcendentals=2 * 1024 * 1664
        ),
    )(
        pinned(activations[0]), pinned(out_grads[0]),
        pinned(weight_scale), pinned(moment_scale), pinned(second_scale),
        pinned(weight_code), pinned(moment_code), pinned(second_code),
    )
    return pl.pallas_call(
        store_kernel,
        out_shape=(
            shape((2048, 1664), BF16), shape((16, 13), F32),
            shape((1024, 1664), BF16), shape((8, 13), F32),
            shape((1024, 1664), BF16), shape((8, 13), F32),
        ),
        in_specs=[vmem] * 5,
        out_specs=(hbm,) * 6,
        scratch_shapes=[
            pltpu.VMEM((16, 13), F32), pltpu.VMEM((8, 13), F32), pltpu.VMEM((8, 13), F32),
            dma((4, 4)), dma((3,)),
        ],
        compiler_params=pltpu.CompilerParams(vmem_limit_bytes=8 << 20),
        cost_estimate=pl.CostEstimate(flops=0, bytes_accessed=26 << 20, transcendentals=0),
    )(*(pltpu.with_memory_space_constraint(x, pltpu.VMEM) for x in held))


def solution(mesh):
    return jax.shard_map(
        per_device,
        mesh=mesh,
        in_specs=(
            P("rep", "row", "col"),
            P("rep", "col", "row"),
            P(("col", "rep"), "row"),
            P(("col", "rep"), "row"),
            P(("col", "rep"), "row"),
            P(("col", "rep"), "row"),
            P(("col", "rep"), "row"),
            P(("col", "rep"), "row"),
        ),
        out_specs=(
            P("col", "row"),
            P("col", "row"),
            P(("col", "rep"), "row"),
            P(("col", "rep"), "row"),
            P(("col", "rep"), "row"),
            P(("col", "rep"), "row"),
        ),
        check_vma=False,
    )
```

```python
import functools

import jax
import jax.numpy as jnp
from jax import lax
from jax.experimental import pallas as pl
from jax.experimental.pallas import tpu as pltpu
from jax.sharding import PartitionSpec as P

MESH = pl.DeviceIdType.MESH
F32 = jnp.float32
BF16 = jnp.bfloat16
CHUNKS = 13
BIAS_ONE = 1.0 - 0.9**10
BIAS_TWO = 1.0 - 0.95**10


def kernel(
    acts_in, grads, w_scale_in, m_scale_in, v_scale_in, w_code, m_code, v_code,
    W, peer_w, M, V, scales,
    acts, A, T, G, acc, new, peak, inv, w_scale, m_scale, v_scale,
    in_sem, own_sem, y_recv, z_recv, zf_recv, sib_recv,
    s1_recv, direct_recv, near_recv, far_recv, w_recv, sc_recv, a_send, g_send, w_send, sc_send,
):
    r, c, p = lax.axis_index("row"), lax.axis_index("col"), lax.axis_index("rep")
    yh, z, k = r // 8, (r // 2) % 4, r % 2
    q, yo = 1 - p, 1 - yh

    def at(yh_, z_, k_, c_, p_):
        return (yh_ * 8 + z_ * 2 + k_, c_, p_)

    partner = at(yh, z, k, c, q)
    other = at(yo, z, k, c, q)
    across = at(yo, z, k, c, p)
    sibling = at(yh, z, 1 - k, c, p)
    z_next, z_prev, z_far = (z + 1) % 4, (z + 3) % 4, (z + 2) % 4
    c_next, c_prev, c_far = (c + 1) % 4, (c + 3) % 4, (c + 2) % 4
    z_dev = (at(yh, z_next, k, c, p), at(yh, z_prev, k, c, p))
    x_dev = (at(yh, z, k, c_next, p), at(yh, z, k, c_prev, p))

    barrier = pltpu.get_barrier_semaphore()
    for device in (partner, other, across, sibling) + z_dev + x_dev:
        pl.semaphore_signal(barrier, inc=1, device_id=device, device_id_type=MESH)

    def remote(src, dst, send, recv, device):
        return pltpu.make_async_remote_copy(
            src_ref=src, dst_ref=dst, send_sem=send, recv_sem=recv,
            device_id=device, device_id_type=MESH,
        )

    def own_rows(part, c_):
        return pl.ds(pl.multiple_of(c_ * 1024 + part * 512, 512), 512)

    def cols(j):
        return pl.ds(pl.multiple_of(j * 128, 128), 128)

    def load_own(j):
        return pltpu.make_async_copy(grads.at[:, cols(j)], G.at[j, own_rows(p, c)], own_sem.at[0])

    def start_own(j, carry):
        load_own(j).start()
        return carry

    lax.fori_loop(0, CHUNKS, start_own, 0)
    loads = [
        pltpu.make_async_copy(w_code, W, in_sem.at[0]),
        pltpu.make_async_copy(m_code, M, in_sem.at[1]),
        pltpu.make_async_copy(v_code, V, in_sem.at[2]),
        pltpu.make_async_copy(w_scale_in, w_scale, in_sem.at[4]),
        pltpu.make_async_copy(m_scale_in, m_scale, in_sem.at[5]),
        pltpu.make_async_copy(v_scale_in, v_scale, in_sem.at[6]),
    ]
    load_acts = pltpu.make_async_copy(acts_in, acts, in_sem.at[3])
    load_acts.start()

    scales[0:24, :] = jnp.zeros((24, 128), F32)
    load_acts.wait()

    def idx(yh_, z_, k_, p_):
        return (yh_ * 2 + z_ // 2) * 8 + p_ * 4 + (z_ % 2) * 2 + k_

    mine = idx(yh, z, k, p)
    for i in range(8):
        A[mine, i * 128:(i + 1) * 128, :] = acts[:, pl.ds(pl.multiple_of(p * 1024 + i * 128, 128), 128)].T
        T[i * 128:(i + 1) * 128, :] = acts[:, pl.ds(pl.multiple_of(q * 1024 + i * 128, 128), 128)].T

    pl.semaphore_wait(barrier, 8)

    piece_yh = (yh, yh, yo, yo)
    piece_p = (p, q, q, p)

    def piece(i, z_, k_):
        return A.at[idx(piece_yh[i], z_, k_, piece_p[i])]

    def y_copy(i):
        src = A.at[mine] if i == 3 else T
        return remote(src, A.at[mine], a_send.at[0], y_recv.at[i], (None, partner, other, across)[i])

    def y_landed(i):
        got = piece(i, z, k)
        return remote(got, got, a_send.at[0], y_recv.at[i], (None, partner, other, across)[i])

    def z_copy(i, d):
        return remote(piece(i, z, k), piece(i, z, k), a_send.at[0], z_recv.at[i], z_dev[d])

    def z_landed(i):
        both = A.at[0:2]
        return remote(both, both, a_send.at[0], z_recv.at[i], z_dev[0])

    def zf_copy(i):
        d = i // 2
        got = piece(i, (z_prev, z_next)[d], k)
        return remote(got, got, a_send.at[0], zf_recv.at[i], z_dev[d])

    def zf_landed(i):
        got = piece(i, z_far, k)
        return remote(got, got, a_send.at[0], zf_recv.at[i], z_dev[i // 2])

    hops = (z, z_prev, z_next, z_far)

    def sib_copy(i, h):
        got = piece(i, hops[h], k)
        return remote(got, got, a_send.at[0], sib_recv.at[0], sibling)

    def sib_landed():
        every = A.at[0:16]
        return remote(every, every, a_send.at[0], sib_recv.at[0], sibling)

    def s1_copy(j):
        rows = G.at[j, own_rows(p, c)]
        return remote(rows, rows, g_send.at[0], s1_recv.at[j], partner)

    def s1_landed(j):
        rows = G.at[j, own_rows(q, c)]
        return remote(rows, rows, g_send.at[0], s1_recv.at[j], partner)

    def sx_copy(j, part, d):
        rows = G.at[j, own_rows((p, q)[part], c)]
        recv = direct_recv if part == d else near_recv
        return remote(rows, rows, g_send.at[0], recv.at[j], x_dev[d])

    def s4_copy(j, d):
        rows = G.at[j, own_rows((p, q)[d], (c_prev, c_next)[d])]
        return remote(rows, rows, g_send.at[0], far_recv.at[j], x_dev[d])

    def pair_landed(j, recv):
        both = G.at[j, 0:1024]
        return remote(both, both, g_send.at[0], recv.at[j], x_dev[0])

    def send_own(j):
        sx_copy(j, 0, 0).start()
        sx_copy(j, 0, 1).start()

    def send_partner(j):
        s1_landed(j).wait_recv()
        sx_copy(j, 1, 0).start()
        sx_copy(j, 1, 1).start()

    def forward(j):
        pair_landed(j, direct_recv).wait_recv()
        s4_copy(j, 0).start()
        s4_copy(j, 1).start()

    def x_step(j):
        forward(j)

        @pl.when(j < 3)
        def _():
            send_partner(j + 3)

        @pl.when(jnp.logical_and(j > 3, j < CHUNKS - 2))
        def _():
            send_partner(j + 2)
            send_own(j + 2)

    def relay(i):
        z_landed(i).wait_recv()
        zf_copy(i).start()
        sib_copy(i, 1).start()
        sib_copy(i, 2).start()

    def spread(i):
        y_landed(i).wait_recv()
        z_copy(i, 0).start()
        z_copy(i, 1).start()
        sib_copy(i, 0).start()

    def finish(i):
        zf_landed(i).wait_recv()
        sib_copy(i, 3).start()

    for i in (1, 2, 3):
        y_copy(i).start()
    z_copy(0, 0).start()
    z_copy(0, 1).start()

    own = G.at[:, own_rows(p, c)]
    pltpu.make_async_copy(own, own, own_sem.at[0]).wait()

    def start_own_sends(j, carry):
        send_own(j)
        return carry

    lax.fori_loop(0, 6, start_own_sends, 0)

    def start_s1(j, carry):
        s1_copy(j).start()
        return carry

    lax.fori_loop(0, CHUNKS, start_s1, 0)
    sib_copy(0, 0).start()
    for load in loads:
        load.start()

    spread(1)
    spread(2)
    relay(0)
    spread(3)
    relay(1)
    send_partner(0)
    send_partner(1)
    relay(2)
    send_partner(2)
    x_step(0)
    x_step(1)
    x_step(2)
    relay(3)
    finish(0)
    finish(2)
    x_step(3)
    x_step(4)
    finish(1)
    finish(3)
    for load in loads:
        load.wait()
    sib_landed().wait_recv()

    lane = lax.broadcasted_iota(jnp.int32, (24, 128), 1)

    def w_copy(j):
        return remote(W.at[:, cols(j)], peer_w.at[:, cols(j)], w_send.at[0], w_recv.at[0], partner)

    sc_copy = remote(scales.at[0:8], scales.at[24:32], sc_send.at[0], sc_recv.at[0], partner)

    def product(j, c_):
        left = jnp.concatenate([A[c_ * 8 + i] for i in range(8)], axis=1)
        right = G[j, pl.ds(pl.multiple_of(c_ * 1024, 1024), 1024), :]
        return jnp.dot(left, right, preferred_element_type=F32)

    def chunk(j, carry):
        @pl.when(jnp.logical_or(j == 1, j == 3))
        def _():
            x_step(5 + j // 2)

        @pl.when(jnp.logical_or(j == 5, jnp.logical_and(j > 6, j < CHUNKS - 1)))
        def _():
            x_step(jnp.where(j == 5, 7, j + 1))

        pair_landed(j, near_recv).wait_recv()
        acc[...] = product(j, c) + product(j, c_prev) + product(j, c_next)
        pair_landed(j, far_recv).wait_recv()
        acc[...] += product(j, c_far)

        def update(d, carry):
            rows = pl.ds(pl.multiple_of(d * 128, 128), 128)
            g = acc[rows, :]
            weight = W[rows, cols(j)].astype(F32) * w_scale[d, j]
            moment = M[rows, cols(j)].astype(F32) * m_scale[d, j]
            second = V[rows, cols(j)].astype(F32) * v_scale[d, j]
            moment1 = 0.9 * moment + 0.1 * g
            second1 = 0.95 * second + 0.05 * (g * g)
            u = second1 * (1.0 / BIAS_TWO)
            denom = u * lax.rsqrt(u) + 1e-08
            weight1 = weight - 0.01 * ((moment1 * (1.0 / BIAS_ONE)) / denom + 0.1 * weight)
            for n, value in enumerate((weight1, moment1, second1)):
                new[n, rows, :] = value
                peak[n * 8 + d] = jnp.max(jnp.abs(value).reshape(16, 8, 128), axis=0)
            return carry

        lax.fori_loop(0, 8, update, 0)
        scale = jnp.max(jnp.max(peak[...], axis=1), axis=1, keepdims=True) + 1e-06
        scale = jnp.broadcast_to(scale, (24, 128))
        scales[0:24, :] = jnp.where(lane == j, scale, scales[0:24, :])
        inv[...] = 1.0 / scale

        @pl.when(j == CHUNKS - 1)
        def _():
            sc_copy.start()

        def encode(d, carry):
            rows = pl.ds(pl.multiple_of(d * 128, 128), 128)
            for n, out in enumerate((W, M, V)):
                out[rows, cols(j)] = (new[n, rows, :] * inv[pl.ds(n * 8 + d, 1), :]).astype(BF16)
            return carry

        lax.fori_loop(0, 8, encode, 0)
        w_copy(j).start()
        return carry

    lax.fori_loop(0, CHUNKS, chunk, 0)

    sent = A.at[0:31]
    remote(sent, sent, a_send.at[0], sib_recv.at[0], sibling).wait_send()
    sent = G.at[:, 0:3584]
    remote(sent, sent, g_send.at[0], s1_recv.at[0], partner).wait_send()
    codes = remote(W, peer_w, w_send.at[0], w_recv.at[0], partner)
    codes.wait_send()
    codes.wait_recv()
    sc_copy.wait()


def store_kernel(W, peer_w, M, V, scales, w_out, ws_out, m_out, ms_out, v_out, vs_out, ws, ms, vs, sem, sc_sem):
    p = lax.axis_index("rep")
    q = 1 - p
    copies = []
    for n in range(4):
        rows = pl.ds(n * 256, 256)
        here = pl.ds(pl.multiple_of(p * 1024 + n * 256, 256), 256)
        there = pl.ds(pl.multiple_of(q * 1024 + n * 256, 256), 256)
        copies += [
            pltpu.make_async_copy(W.at[rows], w_out.at[here], sem.at[0, n]),
            pltpu.make_async_copy(peer_w.at[rows], w_out.at[there], sem.at[1, n]),
            pltpu.make_async_copy(M.at[rows], m_out.at[rows], sem.at[2, n]),
            pltpu.make_async_copy(V.at[rows], v_out.at[rows], sem.at[3, n]),
        ]
    for copy in copies:
        copy.start()
    ws[pl.ds(pl.multiple_of(p * 8, 8), 8), :] = scales[0:8, :CHUNKS]
    ws[pl.ds(pl.multiple_of(q * 8, 8), 8), :] = scales[24:32, :CHUNKS]
    ms[...] = scales[8:16, :CHUNKS]
    vs[...] = scales[16:24, :CHUNKS]
    for n, (src, dst) in enumerate(((ws, ws_out), (ms, ms_out), (vs, vs_out))):
        copies.append(pltpu.make_async_copy(src, dst, sc_sem.at[n]))
        copies[-1].start()
    for copy in copies:
        copy.wait()


def per_device(
    activations, out_grads, weight_code, weight_scale,
    moment_code, moment_scale, second_code, second_scale,
):
    vmem = pl.BlockSpec(memory_space=pltpu.VMEM)
    hbm = pl.BlockSpec(memory_space=pl.ANY)
    dma = pltpu.SemaphoreType.DMA
    shape = jax.ShapeDtypeStruct
    pinned = functools.partial(pltpu.with_memory_space_constraint, memory_space=pltpu.HBM)
    codes = pltpu.VMEM((1024, 1664), BF16)
    held = pl.pallas_call(
        kernel,
        out_shape=(codes, codes, codes, codes, pltpu.VMEM((32, 128), F32)),
        in_specs=[hbm] * 8,
        out_specs=(vmem,) * 5,
        scratch_shapes=[
            pltpu.VMEM((128, 2048), BF16),
            pltpu.VMEM((32, 1024, 128), BF16),
            pltpu.VMEM((1024, 128), BF16),
            pltpu.VMEM((CHUNKS, 4096, 128), BF16),
            pltpu.VMEM((1024, 128), F32),
            pltpu.VMEM((3, 1024, 128), F32),
            pltpu.VMEM((24, 8, 128), F32),
            pltpu.VMEM((24, 128), F32),
            pltpu.SMEM((8, 13), F32),
            pltpu.SMEM((8, 13), F32),
            pltpu.SMEM((8, 13), F32),
            dma((7,)), dma((1,)), dma((4,)), dma((4,)), dma((4,)), dma((1,)),
            dma((CHUNKS,)), dma((CHUNKS,)), dma((CHUNKS,)), dma((CHUNKS,)), dma((1,)), dma((1,)),
            dma((1,)), dma((1,)), dma((1,)), dma((1,)),
        ],
        compiler_params=pltpu.CompilerParams(
            collective_id=0, has_side_effects=True, vmem_limit_bytes=32 << 20
        ),
        cost_estimate=pl.CostEstimate(
            flops=2 * 1024 * 1664 * 4096, bytes_accessed=26 << 20, transcendentals=2 * 1024 * 1664
        ),
    )(
        pinned(activations[0]), pinned(out_grads[0]),
        pinned(weight_scale), pinned(moment_scale), pinned(second_scale),
        pinned(weight_code), pinned(moment_code), pinned(second_code),
    )
    return pl.pallas_call(
        store_kernel,
        out_shape=(
            shape((2048, 1664), BF16), shape((16, 13), F32),
            shape((1024, 1664), BF16), shape((8, 13), F32),
            shape((1024, 1664), BF16), shape((8, 13), F32),
        ),
        in_specs=[vmem] * 5,
        out_specs=(hbm,) * 6,
        scratch_shapes=[
            pltpu.VMEM((16, 13), F32), pltpu.VMEM((8, 13), F32), pltpu.VMEM((8, 13), F32),
            dma((4, 4)), dma((3,)),
        ],
        compiler_params=pltpu.CompilerParams(vmem_limit_bytes=8 << 20),
        cost_estimate=pl.CostEstimate(flops=0, bytes_accessed=26 << 20, transcendentals=0),
    )(*(pltpu.with_memory_space_constraint(x, pltpu.VMEM) for x in held))


def solution(mesh):
    return jax.shard_map(
        per_device,
        mesh=mesh,
        in_specs=(
            P("rep", "row", "col"),
            P("rep", "col", "row"),
            P(("col", "rep"), "row"),
            P(("col", "rep"), "row"),
            P(("col", "rep"), "row"),
            P(("col", "rep"), "row"),
            P(("col", "rep"), "row"),
            P(("col", "rep"), "row"),
        ),
        out_specs=(
            P("col", "row"),
            P("col", "row"),
            P(("col", "rep"), "row"),
            P(("col", "rep"), "row"),
            P(("col", "rep"), "row"),
            P(("col", "rep"), "row"),
        ),
        check_vma=False,
    )
```

```python
import functools

import jax
import jax.numpy as jnp
from jax import lax
from jax.experimental import pallas as pl
from jax.experimental.pallas import tpu as pltpu
from jax.sharding import PartitionSpec as P

MESH = pl.DeviceIdType.MESH
F32 = jnp.float32
BF16 = jnp.bfloat16
CHUNKS = 13
BIAS_ONE = 1.0 - 0.9**10
BIAS_TWO = 1.0 - 0.95**10


def kernel(
    acts_in, grads, w_scale_in, m_scale_in, v_scale_in, w_code, m_code, v_code,
    W, peer_w, M, V, scales,
    acts, A, T, G, acc, new, peak, inv, w_scale, m_scale, v_scale,
    in_sem, own_sem, y_recv, z_recv, zf_recv, sib_recv,
    s1_recv, direct_recv, near_recv, far_recv, w_recv, sc_recv, a_send, g_send, w_send, sc_send,
):
    r, c, p = lax.axis_index("row"), lax.axis_index("col"), lax.axis_index("rep")
    yh, z, k = r // 8, (r // 2) % 4, r % 2
    q, yo = 1 - p, 1 - yh

    def at(yh_, z_, k_, c_, p_):
        return (yh_ * 8 + z_ * 2 + k_, c_, p_)

    partner = at(yh, z, k, c, q)
    other = at(yo, z, k, c, q)
    across = at(yo, z, k, c, p)
    sibling = at(yh, z, 1 - k, c, p)
    z_next, z_prev, z_far = (z + 1) % 4, (z + 3) % 4, (z + 2) % 4
    c_next, c_prev, c_far = (c + 1) % 4, (c + 3) % 4, (c + 2) % 4
    z_dev = (at(yh, z_next, k, c, p), at(yh, z_prev, k, c, p))
    x_dev = (at(yh, z, k, c_next, p), at(yh, z, k, c_prev, p))

    barrier = pltpu.get_barrier_semaphore()
    for device in (partner, other, across, sibling) + z_dev + x_dev:
        pl.semaphore_signal(barrier, inc=1, device_id=device, device_id_type=MESH)

    def remote(src, dst, send, recv, device):
        return pltpu.make_async_remote_copy(
            src_ref=src, dst_ref=dst, send_sem=send, recv_sem=recv,
            device_id=device, device_id_type=MESH,
        )

    def own_rows(part, c_):
        return pl.ds(pl.multiple_of(c_ * 1024 + part * 512, 512), 512)

    def cols(j):
        return pl.ds(pl.multiple_of(j * 128, 128), 128)

    def load_own(j):
        return pltpu.make_async_copy(grads.at[:, cols(j)], G.at[j, own_rows(p, c)], own_sem.at[0])

    load_acts = pltpu.make_async_copy(acts_in, acts, in_sem.at[3])
    load_acts.start()

    def start_own(j, carry):
        load_own(j).start()
        return carry

    lax.fori_loop(0, CHUNKS, start_own, 0)
    loads = [
        pltpu.make_async_copy(w_code, W, in_sem.at[0]),
        pltpu.make_async_copy(m_code, M, in_sem.at[1]),
        pltpu.make_async_copy(v_code, V, in_sem.at[2]),
        pltpu.make_async_copy(w_scale_in, w_scale, in_sem.at[4]),
        pltpu.make_async_copy(m_scale_in, m_scale, in_sem.at[5]),
        pltpu.make_async_copy(v_scale_in, v_scale, in_sem.at[6]),
    ]

    scales[0:24, :] = jnp.zeros((24, 128), F32)
    load_acts.wait()

    def idx(yh_, z_, k_, p_):
        return (yh_ * 2 + z_ // 2) * 8 + p_ * 4 + (z_ % 2) * 2 + k_

    mine = idx(yh, z, k, p)
    for i in range(8):
        A[mine, i * 128:(i + 1) * 128, :] = acts[:, pl.ds(pl.multiple_of(p * 1024 + i * 128, 128), 128)].T
        T[i * 128:(i + 1) * 128, :] = acts[:, pl.ds(pl.multiple_of(q * 1024 + i * 128, 128), 128)].T

    pl.semaphore_wait(barrier, 8)

    piece_yh = (yh, yh, yo, yo)
    piece_p = (p, q, q, p)

    def piece(i, z_, k_):
        return A.at[idx(piece_yh[i], z_, k_, piece_p[i])]

    def y_copy(i):
        src = A.at[mine] if i == 3 else T
        return remote(src, A.at[mine], a_send.at[0], y_recv.at[i], (None, partner, other, across)[i])

    def y_landed(i):
        got = piece(i, z, k)
        return remote(got, got, a_send.at[0], y_recv.at[i], (None, partner, other, across)[i])

    def z_copy(i, d):
        return remote(piece(i, z, k), piece(i, z, k), a_send.at[0], z_recv.at[i], z_dev[d])

    def z_landed(i):
        both = A.at[0:2]
        return remote(both, both, a_send.at[0], z_recv.at[i], z_dev[0])

    def zf_copy(i):
        d = i // 2
        got = piece(i, (z_prev, z_next)[d], k)
        return remote(got, got, a_send.at[0], zf_recv.at[i], z_dev[d])

    def zf_landed(i):
        got = piece(i, z_far, k)
        return remote(got, got, a_send.at[0], zf_recv.at[i], z_dev[i // 2])

    hops = (z, z_prev, z_next, z_far)

    def sib_copy(i, h):
        got = piece(i, hops[h], k)
        return remote(got, got, a_send.at[0], sib_recv.at[0], sibling)

    def sib_landed():
        every = A.at[0:16]
        return remote(every, every, a_send.at[0], sib_recv.at[0], sibling)

    def s1_copy(j):
        rows = G.at[j, own_rows(p, c)]
        return remote(rows, rows, g_send.at[0], s1_recv.at[j], partner)

    def s1_landed(j):
        rows = G.at[j, own_rows(q, c)]
        return remote(rows, rows, g_send.at[0], s1_recv.at[j], partner)

    def sx_copy(j, part, d):
        rows = G.at[j, own_rows((p, q)[part], c)]
        recv = direct_recv if part == d else near_recv
        return remote(rows, rows, g_send.at[0], recv.at[j], x_dev[d])

    def s4_copy(j, d):
        rows = G.at[j, own_rows((p, q)[d], (c_prev, c_next)[d])]
        return remote(rows, rows, g_send.at[0], far_recv.at[j], x_dev[d])

    def pair_landed(j, recv):
        both = G.at[j, 0:1024]
        return remote(both, both, g_send.at[0], recv.at[j], x_dev[0])

    def send_own(j):
        sx_copy(j, 0, 0).start()
        sx_copy(j, 0, 1).start()

    def send_partner(j):
        s1_landed(j).wait_recv()
        sx_copy(j, 1, 0).start()
        sx_copy(j, 1, 1).start()

    def send_direct(j):
        sx_copy(j, 0, 0).start()
        sx_copy(j, 1, 1).start()

    def send_near(j):
        sx_copy(j, 1, 0).start()
        sx_copy(j, 0, 1).start()

    def forward(j):
        pair_landed(j, direct_recv).wait_recv()
        s4_copy(j, 0).start()
        s4_copy(j, 1).start()

    def x_step(j):
        forward(j)

        @pl.when(j < 3)
        def _():
            send_partner(j + 3)

        @pl.when(jnp.logical_and(j > 3, j < CHUNKS - 2))
        def _():
            s1_landed(j + 2).wait_recv()
            send_direct(j + 2)

        @pl.when(jnp.logical_and(j > 3, j < CHUNKS - 3))
        def _():
            send_near(j + 2)

        @pl.when(j == CHUNKS - 2)
        def _():
            send_near(j + 1)

    def relay(i):
        z_landed(i).wait_recv()
        zf_copy(i).start()
        sib_copy(i, 1).start()
        sib_copy(i, 2).start()

    def spread(i):
        y_landed(i).wait_recv()
        z_copy(i, 0).start()
        z_copy(i, 1).start()
        sib_copy(i, 0).start()

    def finish(i):
        zf_landed(i).wait_recv()
        sib_copy(i, 3).start()

    for i in (1, 2, 3):
        y_copy(i).start()
    own = G.at[:, own_rows(p, c)]
    pltpu.make_async_copy(own, own, own_sem.at[0]).wait()

    send_own(0)
    z_copy(0, 0).start()
    z_copy(0, 1).start()

    def start_own_sends(j, carry):
        send_own(j)
        return carry

    lax.fori_loop(1, 6, start_own_sends, 0)

    def start_s1(j, carry):
        s1_copy(j).start()
        return carry

    lax.fori_loop(0, CHUNKS, start_s1, 0)
    sib_copy(0, 0).start()
    for load in loads:
        load.start()

    spread(1)
    spread(2)
    relay(0)
    spread(3)
    relay(1)
    send_partner(0)
    send_partner(1)
    relay(2)
    send_partner(2)
    x_step(0)
    x_step(1)
    x_step(2)
    relay(3)
    finish(0)
    finish(2)
    x_step(3)
    x_step(4)
    finish(1)
    finish(3)
    for load in loads:
        load.wait()
    sib_landed().wait_recv()

    lane = lax.broadcasted_iota(jnp.int32, (24, 128), 1)

    def w_copy(j):
        return remote(W.at[:, cols(j)], peer_w.at[:, cols(j)], w_send.at[0], w_recv.at[0], partner)

    sc_copy = remote(scales.at[0:8], scales.at[24:32], sc_send.at[0], sc_recv.at[0], partner)

    def product(j, c_):
        left = jnp.concatenate([A[c_ * 8 + i] for i in range(8)], axis=1)
        right = G[j, pl.ds(pl.multiple_of(c_ * 1024, 1024), 1024), :]
        return jnp.dot(left, right, preferred_element_type=F32)

    def chunk(j, carry):
        @pl.when(jnp.logical_or(j == 1, j == 3))
        def _():
            x_step(5 + j // 2)

        @pl.when(jnp.logical_or(j == 5, jnp.logical_and(j > 6, j < CHUNKS - 1)))
        def _():
            x_step(jnp.where(j == 5, 7, j + 1))

        pair_landed(j, near_recv).wait_recv()
        acc[...] = product(j, c) + product(j, c_prev) + product(j, c_next)
        pair_landed(j, far_recv).wait_recv()
        acc[...] += product(j, c_far)

        def update(d, carry):
            rows = pl.ds(pl.multiple_of(d * 128, 128), 128)
            g = acc[rows, :]
            weight = W[rows, cols(j)].astype(F32) * w_scale[d, j]
            moment = M[rows, cols(j)].astype(F32) * m_scale[d, j]
            second = V[rows, cols(j)].astype(F32) * v_scale[d, j]
            moment1 = 0.9 * moment + 0.1 * g
            second1 = 0.95 * second + 0.05 * (g * g)
            u = second1 * (1.0 / BIAS_TWO)
            denom = u * lax.rsqrt(u) + 1e-08
            weight1 = weight - 0.01 * ((moment1 * (1.0 / BIAS_ONE)) / denom + 0.1 * weight)
            for n, value in enumerate((weight1, moment1, second1)):
                new[n, rows, :] = value
                peak[n * 8 + d] = jnp.max(jnp.abs(value).reshape(16, 8, 128), axis=0)
            return carry

        lax.fori_loop(0, 8, update, 0)
        scale = jnp.max(jnp.max(peak[...], axis=1), axis=1, keepdims=True) + 1e-06
        scale = jnp.broadcast_to(scale, (24, 128))
        scales[0:24, :] = jnp.where(lane == j, scale, scales[0:24, :])
        inv[...] = 1.0 / scale

        @pl.when(j == CHUNKS - 1)
        def _():
            sc_copy.start()

        def encode(d, carry):
            rows = pl.ds(pl.multiple_of(d * 128, 128), 128)
            for n, out in enumerate((W, M, V)):
                out[rows, cols(j)] = (new[n, rows, :] * inv[pl.ds(n * 8 + d, 1), :]).astype(BF16)
            return carry

        lax.fori_loop(0, 8, encode, 0)
        w_copy(j).start()
        return carry

    lax.fori_loop(0, CHUNKS, chunk, 0)

    sent = A.at[0:31]
    remote(sent, sent, a_send.at[0], sib_recv.at[0], sibling).wait_send()
    sent = G.at[:, 0:3584]
    remote(sent, sent, g_send.at[0], s1_recv.at[0], partner).wait_send()
    codes = remote(W, peer_w, w_send.at[0], w_recv.at[0], partner)
    codes.wait_send()
    codes.wait_recv()
    sc_copy.wait()


def store_kernel(W, peer_w, M, V, scales, w_out, ws_out, m_out, ms_out, v_out, vs_out, ws, ms, vs, sem, sc_sem):
    p = lax.axis_index("rep")
    q = 1 - p
    copies = []
    for n in range(4):
        rows = pl.ds(n * 256, 256)
        here = pl.ds(pl.multiple_of(p * 1024 + n * 256, 256), 256)
        there = pl.ds(pl.multiple_of(q * 1024 + n * 256, 256), 256)
        copies += [
            pltpu.make_async_copy(W.at[rows], w_out.at[here], sem.at[0, n]),
            pltpu.make_async_copy(peer_w.at[rows], w_out.at[there], sem.at[1, n]),
            pltpu.make_async_copy(M.at[rows], m_out.at[rows], sem.at[2, n]),
            pltpu.make_async_copy(V.at[rows], v_out.at[rows], sem.at[3, n]),
        ]
    for copy in copies:
        copy.start()
    ws[pl.ds(pl.multiple_of(p * 8, 8), 8), :] = scales[0:8, :CHUNKS]
    ws[pl.ds(pl.multiple_of(q * 8, 8), 8), :] = scales[24:32, :CHUNKS]
    ms[...] = scales[8:16, :CHUNKS]
    vs[...] = scales[16:24, :CHUNKS]
    for n, (src, dst) in enumerate(((ws, ws_out), (ms, ms_out), (vs, vs_out))):
        copies.append(pltpu.make_async_copy(src, dst, sc_sem.at[n]))
        copies[-1].start()
    for copy in copies:
        copy.wait()


def per_device(
    activations, out_grads, weight_code, weight_scale,
    moment_code, moment_scale, second_code, second_scale,
):
    vmem = pl.BlockSpec(memory_space=pltpu.VMEM)
    hbm = pl.BlockSpec(memory_space=pl.ANY)
    dma = pltpu.SemaphoreType.DMA
    shape = jax.ShapeDtypeStruct
    pinned = functools.partial(pltpu.with_memory_space_constraint, memory_space=pltpu.HBM)
    codes = pltpu.VMEM((1024, 1664), BF16)
    held = pl.pallas_call(
        kernel,
        out_shape=(codes, codes, codes, codes, pltpu.VMEM((32, 128), F32)),
        in_specs=[hbm] * 8,
        out_specs=(vmem,) * 5,
        scratch_shapes=[
            pltpu.VMEM((128, 2048), BF16),
            pltpu.VMEM((32, 1024, 128), BF16),
            pltpu.VMEM((1024, 128), BF16),
            pltpu.VMEM((CHUNKS, 4096, 128), BF16),
            pltpu.VMEM((1024, 128), F32),
            pltpu.VMEM((3, 1024, 128), F32),
            pltpu.VMEM((24, 8, 128), F32),
            pltpu.VMEM((24, 128), F32),
            pltpu.SMEM((8, 13), F32),
            pltpu.SMEM((8, 13), F32),
            pltpu.SMEM((8, 13), F32),
            dma((7,)), dma((1,)), dma((4,)), dma((4,)), dma((4,)), dma((1,)),
            dma((CHUNKS,)), dma((CHUNKS,)), dma((CHUNKS,)), dma((CHUNKS,)), dma((1,)), dma((1,)),
            dma((1,)), dma((1,)), dma((1,)), dma((1,)),
        ],
        compiler_params=pltpu.CompilerParams(
            collective_id=0, has_side_effects=True, vmem_limit_bytes=32 << 20
        ),
        cost_estimate=pl.CostEstimate(
            flops=2 * 1024 * 1664 * 4096, bytes_accessed=26 << 20, transcendentals=2 * 1024 * 1664
        ),
    )(
        pinned(activations[0]), pinned(out_grads[0]),
        pinned(weight_scale), pinned(moment_scale), pinned(second_scale),
        pinned(weight_code), pinned(moment_code), pinned(second_code),
    )
    return pl.pallas_call(
        store_kernel,
        out_shape=(
            shape((2048, 1664), BF16), shape((16, 13), F32),
            shape((1024, 1664), BF16), shape((8, 13), F32),
            shape((1024, 1664), BF16), shape((8, 13), F32),
        ),
        in_specs=[vmem] * 5,
        out_specs=(hbm,) * 6,
        scratch_shapes=[
            pltpu.VMEM((16, 13), F32), pltpu.VMEM((8, 13), F32), pltpu.VMEM((8, 13), F32),
            dma((4, 4)), dma((3,)),
        ],
        compiler_params=pltpu.CompilerParams(vmem_limit_bytes=8 << 20),
        cost_estimate=pl.CostEstimate(flops=0, bytes_accessed=26 << 20, transcendentals=0),
    )(*(pltpu.with_memory_space_constraint(x, pltpu.VMEM) for x in held))


def solution(mesh):
    return jax.shard_map(
        per_device,
        mesh=mesh,
        in_specs=(
            P("rep", "row", "col"),
            P("rep", "col", "row"),
            P(("col", "rep"), "row"),
            P(("col", "rep"), "row"),
            P(("col", "rep"), "row"),
            P(("col", "rep"), "row"),
            P(("col", "rep"), "row"),
            P(("col", "rep"), "row"),
        ),
        out_specs=(
            P("col", "row"),
            P("col", "row"),
            P(("col", "rep"), "row"),
            P(("col", "rep"), "row"),
            P(("col", "rep"), "row"),
            P(("col", "rep"), "row"),
        ),
        check_vma=False,
    )
```

```python
import functools

import jax
import jax.numpy as jnp
from jax import lax
from jax.experimental import pallas as pl
from jax.experimental.pallas import tpu as pltpu
from jax.sharding import PartitionSpec as P

MESH = pl.DeviceIdType.MESH
F32 = jnp.float32
BF16 = jnp.bfloat16
CHUNKS = 13
MOST = 12 * 128
BIAS_ONE = 1.0 - 0.9**10
BIAS_TWO = 1.0 - 0.95**10


def kernel(
    acts_in, grads, w_scale_in, m_scale_in, v_scale_in, w_code, m_code, v_code,
    W, peer_w, M, V, scales, last,
    acts, A, T, G, acc, new, peak, inv, w_scale, m_scale, v_scale,
    in_sem, own_sem, y_recv, z_recv, zf_recv, sib_recv,
    s1_recv, direct_recv, near_recv, far_recv, w_recv, sc_recv, a_send, g_send, w_send, sc_send,
):
    r, c, p = lax.axis_index("row"), lax.axis_index("col"), lax.axis_index("rep")
    yh, z, k = r // 8, (r // 2) % 4, r % 2
    q, yo = 1 - p, 1 - yh

    def at(yh_, z_, k_, c_, p_):
        return (yh_ * 8 + z_ * 2 + k_, c_, p_)

    partner = at(yh, z, k, c, q)
    other = at(yo, z, k, c, q)
    across = at(yo, z, k, c, p)
    sibling = at(yh, z, 1 - k, c, p)
    z_next, z_prev, z_far = (z + 1) % 4, (z + 3) % 4, (z + 2) % 4
    c_next, c_prev, c_far = (c + 1) % 4, (c + 3) % 4, (c + 2) % 4
    z_dev = (at(yh, z_next, k, c, p), at(yh, z_prev, k, c, p))
    x_dev = (at(yh, z, k, c_next, p), at(yh, z, k, c_prev, p))

    barrier = pltpu.get_barrier_semaphore()
    for device in (partner, other, across, sibling) + z_dev + x_dev:
        pl.semaphore_signal(barrier, inc=1, device_id=device, device_id_type=MESH)

    def remote(src, dst, send, recv, device):
        return pltpu.make_async_remote_copy(
            src_ref=src, dst_ref=dst, send_sem=send, recv_sem=recv,
            device_id=device, device_id_type=MESH,
        )

    def own_rows(part, c_):
        return pl.ds(pl.multiple_of(c_ * 1024 + part * 512, 512), 512)

    def cols(j):
        return pl.ds(pl.multiple_of(j * 128, 128), 128)

    def load_own(j):
        return pltpu.make_async_copy(grads.at[:, cols(j)], G.at[j, own_rows(p, c)], own_sem.at[0])

    load_acts = pltpu.make_async_copy(acts_in, acts, in_sem.at[3])
    load_acts.start()

    def start_own(j, carry):
        load_own(j).start()
        return carry

    lax.fori_loop(0, CHUNKS, start_own, 0)
    loads = [
        pltpu.make_async_copy(w_code, W, in_sem.at[0]),
        pltpu.make_async_copy(m_code, M, in_sem.at[1]),
        pltpu.make_async_copy(v_code, V, in_sem.at[2]),
        pltpu.make_async_copy(w_scale_in, w_scale, in_sem.at[4]),
        pltpu.make_async_copy(m_scale_in, m_scale, in_sem.at[5]),
        pltpu.make_async_copy(v_scale_in, v_scale, in_sem.at[6]),
    ]

    scales[0:24, :] = jnp.zeros((24, 128), F32)
    load_acts.wait()

    def idx(yh_, z_, k_, p_):
        return (yh_ * 2 + z_ // 2) * 8 + p_ * 4 + (z_ % 2) * 2 + k_

    mine = idx(yh, z, k, p)
    for i in range(8):
        A[mine, i * 128:(i + 1) * 128, :] = acts[:, pl.ds(pl.multiple_of(p * 1024 + i * 128, 128), 128)].T
        T[i * 128:(i + 1) * 128, :] = acts[:, pl.ds(pl.multiple_of(q * 1024 + i * 128, 128), 128)].T

    pl.semaphore_wait(barrier, 8)

    piece_yh = (yh, yh, yo, yo)
    piece_p = (p, q, q, p)

    def piece(i, z_, k_):
        return A.at[idx(piece_yh[i], z_, k_, piece_p[i])]

    def y_copy(i):
        src = A.at[mine] if i == 3 else T
        return remote(src, A.at[mine], a_send.at[0], y_recv.at[i], (None, partner, other, across)[i])

    def y_landed(i):
        got = piece(i, z, k)
        return remote(got, got, a_send.at[0], y_recv.at[i], (None, partner, other, across)[i])

    def z_copy(i, d):
        return remote(piece(i, z, k), piece(i, z, k), a_send.at[0], z_recv.at[i], z_dev[d])

    def z_landed(i):
        both = A.at[0:2]
        return remote(both, both, a_send.at[0], z_recv.at[i], z_dev[0])

    def zf_copy(i):
        d = i // 2
        got = piece(i, (z_prev, z_next)[d], k)
        return remote(got, got, a_send.at[0], zf_recv.at[i], z_dev[d])

    def zf_landed(i):
        got = piece(i, z_far, k)
        return remote(got, got, a_send.at[0], zf_recv.at[i], z_dev[i // 2])

    hops = (z, z_prev, z_next, z_far)

    def sib_copy(i, h):
        got = piece(i, hops[h], k)
        return remote(got, got, a_send.at[0], sib_recv.at[0], sibling)

    def sib_landed():
        every = A.at[0:16]
        return remote(every, every, a_send.at[0], sib_recv.at[0], sibling)

    def s1_copy(j):
        rows = G.at[j, own_rows(p, c)]
        return remote(rows, rows, g_send.at[0], s1_recv.at[j], partner)

    def s1_landed(j):
        rows = G.at[j, own_rows(q, c)]
        return remote(rows, rows, g_send.at[0], s1_recv.at[j], partner)

    def sx_copy(j, part, d):
        rows = G.at[j, own_rows((p, q)[part], c)]
        recv = direct_recv if part == d else near_recv
        return remote(rows, rows, g_send.at[0], recv.at[j], x_dev[d])

    def s4_copy(j, d):
        rows = G.at[j, own_rows((p, q)[d], (c_prev, c_next)[d])]
        return remote(rows, rows, g_send.at[0], far_recv.at[j], x_dev[d])

    def pair_landed(j, recv):
        both = G.at[j, 0:1024]
        return remote(both, both, g_send.at[0], recv.at[j], x_dev[0])

    def send_own(j):
        sx_copy(j, 0, 0).start()
        sx_copy(j, 0, 1).start()

    def send_partner(j):
        s1_landed(j).wait_recv()
        sx_copy(j, 1, 0).start()
        sx_copy(j, 1, 1).start()

    def send_direct(j):
        sx_copy(j, 0, 0).start()
        sx_copy(j, 1, 1).start()

    def send_near(j):
        sx_copy(j, 1, 0).start()
        sx_copy(j, 0, 1).start()

    def forward(j):
        pair_landed(j, direct_recv).wait_recv()
        s4_copy(j, 0).start()
        s4_copy(j, 1).start()

    def x_step(j):
        forward(j)

        @pl.when(j < 3)
        def _():
            send_partner(j + 3)

        @pl.when(jnp.logical_and(j > 3, j < CHUNKS - 2))
        def _():
            s1_landed(j + 2).wait_recv()
            send_direct(j + 2)

        @pl.when(jnp.logical_and(j > 3, j < CHUNKS - 3))
        def _():
            send_near(j + 2)

        @pl.when(j == CHUNKS - 2)
        def _():
            send_near(j + 1)

    def relay(i):
        z_landed(i).wait_recv()
        zf_copy(i).start()
        sib_copy(i, 1).start()
        sib_copy(i, 2).start()

    def spread(i):
        y_landed(i).wait_recv()
        z_copy(i, 0).start()
        z_copy(i, 1).start()
        sib_copy(i, 0).start()

    def finish(i):
        zf_landed(i).wait_recv()
        sib_copy(i, 3).start()

    for i in (1, 2, 3):
        y_copy(i).start()
    own = G.at[:, own_rows(p, c)]
    pltpu.make_async_copy(own, own, own_sem.at[0]).wait()

    send_own(0)
    z_copy(0, 0).start()
    z_copy(0, 1).start()

    def start_own_sends(j, carry):
        send_own(j)
        return carry

    lax.fori_loop(1, 6, start_own_sends, 0)

    def start_s1(j, carry):
        s1_copy(j).start()
        return carry

    lax.fori_loop(0, CHUNKS, start_s1, 0)
    sib_copy(0, 0).start()
    for load in loads:
        load.start()

    spread(1)
    spread(2)
    relay(0)
    spread(3)
    relay(1)
    send_partner(0)
    send_partner(1)
    relay(2)
    send_partner(2)
    x_step(0)
    x_step(1)
    x_step(2)
    relay(3)
    finish(0)
    finish(2)
    x_step(3)
    x_step(4)
    finish(1)
    finish(3)
    for load in loads:
        load.wait()
    sib_landed().wait_recv()

    lane = lax.broadcasted_iota(jnp.int32, (24, 128), 1)

    def w_copy(j):
        return remote(W.at[:, cols(j)], peer_w.at[:, cols(j)], w_send.at[0], w_recv.at[0], partner)

    sc_copy = remote(scales.at[0:8], scales.at[24:32], sc_send.at[0], sc_recv.at[0], partner)

    keep_last = pltpu.make_async_copy(W.at[:, MOST:], last, in_sem.at[3])

    def product(j, c_):
        left = jnp.concatenate([A[c_ * 8 + i] for i in range(8)], axis=1)
        right = G[j, pl.ds(pl.multiple_of(c_ * 1024, 1024), 1024), :]
        return jnp.dot(left, right, preferred_element_type=F32)

    def chunk(j, carry):
        @pl.when(jnp.logical_or(j == 1, j == 3))
        def _():
            x_step(5 + j // 2)

        @pl.when(jnp.logical_or(j == 5, jnp.logical_and(j > 6, j < CHUNKS - 1)))
        def _():
            x_step(jnp.where(j == 5, 7, j + 1))

        pair_landed(j, near_recv).wait_recv()
        acc[...] = product(j, c) + product(j, c_prev) + product(j, c_next)
        pair_landed(j, far_recv).wait_recv()
        acc[...] += product(j, c_far)

        def update(d, carry):
            rows = pl.ds(pl.multiple_of(d * 128, 128), 128)
            g = acc[rows, :]
            weight = W[rows, cols(j)].astype(F32) * w_scale[d, j]
            moment = M[rows, cols(j)].astype(F32) * m_scale[d, j]
            second = V[rows, cols(j)].astype(F32) * v_scale[d, j]
            moment1 = 0.9 * moment + 0.1 * g
            second1 = 0.95 * second + 0.05 * (g * g)
            u = second1 * (1.0 / BIAS_TWO)
            denom = u * lax.rsqrt(u) + 1e-08
            weight1 = weight - 0.01 * ((moment1 * (1.0 / BIAS_ONE)) / denom + 0.1 * weight)
            for n, value in enumerate((weight1, moment1, second1)):
                new[n, rows, :] = value
                peak[n * 8 + d] = jnp.max(jnp.abs(value).reshape(16, 8, 128), axis=0)
            return carry

        lax.fori_loop(0, 8, update, 0)
        scale = jnp.max(jnp.max(peak[...], axis=1), axis=1, keepdims=True) + 1e-06
        scale = jnp.broadcast_to(scale, (24, 128))
        scales[0:24, :] = jnp.where(lane == j, scale, scales[0:24, :])
        inv[...] = 1.0 / scale

        @pl.when(j == CHUNKS - 1)
        def _():
            sc_copy.start()

        def encode(d, carry):
            rows = pl.ds(pl.multiple_of(d * 128, 128), 128)
            for n, out in enumerate((W, M, V)):
                out[rows, cols(j)] = (new[n, rows, :] * inv[pl.ds(n * 8 + d, 1), :]).astype(BF16)
            return carry

        lax.fori_loop(0, 8, encode, 0)
        @pl.when(j < CHUNKS - 1)
        def _():
            w_copy(j).start()

        @pl.when(j == CHUNKS - 1)
        def _():
            keep_last.start()

        return carry

    lax.fori_loop(0, CHUNKS, chunk, 0)

    sent = A.at[0:31]
    remote(sent, sent, a_send.at[0], sib_recv.at[0], sibling).wait_send()
    sent = G.at[:, 0:3584]
    remote(sent, sent, g_send.at[0], s1_recv.at[0], partner).wait_send()
    keep_last.wait()
    codes = remote(W.at[:, :MOST], peer_w.at[:, :MOST], w_send.at[0], w_recv.at[0], partner)
    codes.wait_send()
    codes.wait_recv()
    sc_copy.wait()


def store_kernel(W, peer_w, M, V, scales, w_out, ws_out, m_out, ms_out, v_out, vs_out, ws, ms, vs, sem, sc_sem):
    p = lax.axis_index("rep")
    q = 1 - p
    copies = []
    for n in range(4):
        rows = pl.ds(n * 256, 256)
        here = pl.ds(pl.multiple_of(p * 1024 + n * 256, 256), 256)
        there = pl.ds(pl.multiple_of(q * 1024 + n * 256, 256), 256)
        copies += [
            pltpu.make_async_copy(W.at[rows], w_out.at[here], sem.at[0, n]),
            pltpu.make_async_copy(peer_w.at[rows, :MOST], w_out.at[there, :MOST], sem.at[1, n]),
            pltpu.make_async_copy(M.at[rows], m_out.at[rows], sem.at[2, n]),
            pltpu.make_async_copy(V.at[rows], v_out.at[rows], sem.at[3, n]),
        ]
    for copy in copies:
        copy.start()
    ws[pl.ds(pl.multiple_of(p * 8, 8), 8), :] = scales[0:8, :CHUNKS]
    ws[pl.ds(pl.multiple_of(q * 8, 8), 8), :] = scales[24:32, :CHUNKS]
    ms[...] = scales[8:16, :CHUNKS]
    vs[...] = scales[16:24, :CHUNKS]
    for n, (src, dst) in enumerate(((ws, ws_out), (ms, ms_out), (vs, vs_out))):
        copies.append(pltpu.make_async_copy(src, dst, sc_sem.at[n]))
        copies[-1].start()
    for copy in copies:
        copy.wait()


def last_kernel(_, peer_last, w_out, sem):
    there = pl.ds(pl.multiple_of((1 - lax.axis_index("rep")) * 1024, 1024), 1024)
    copy = pltpu.make_async_copy(peer_last, w_out.at[there, MOST:], sem.at[0])
    copy.start()
    copy.wait()


def per_device(
    activations, out_grads, weight_code, weight_scale,
    moment_code, moment_scale, second_code, second_scale,
):
    vmem = pl.BlockSpec(memory_space=pltpu.VMEM)
    hbm = pl.BlockSpec(memory_space=pl.ANY)
    dma = pltpu.SemaphoreType.DMA
    shape = jax.ShapeDtypeStruct
    pinned = functools.partial(pltpu.with_memory_space_constraint, memory_space=pltpu.HBM)
    codes = pltpu.VMEM((1024, 1664), BF16)
    *held, last = pl.pallas_call(
        kernel,
        out_shape=(codes, codes, codes, codes, pltpu.VMEM((32, 128), F32), shape((1024, 128), BF16)),
        in_specs=[hbm] * 8,
        out_specs=(vmem,) * 5 + (hbm,),
        scratch_shapes=[
            pltpu.VMEM((128, 2048), BF16),
            pltpu.VMEM((32, 1024, 128), BF16),
            pltpu.VMEM((1024, 128), BF16),
            pltpu.VMEM((CHUNKS, 4096, 128), BF16),
            pltpu.VMEM((1024, 128), F32),
            pltpu.VMEM((3, 1024, 128), F32),
            pltpu.VMEM((24, 8, 128), F32),
            pltpu.VMEM((24, 128), F32),
            pltpu.SMEM((8, 13), F32),
            pltpu.SMEM((8, 13), F32),
            pltpu.SMEM((8, 13), F32),
            dma((7,)), dma((1,)), dma((4,)), dma((4,)), dma((4,)), dma((1,)),
            dma((CHUNKS,)), dma((CHUNKS,)), dma((CHUNKS,)), dma((CHUNKS,)), dma((1,)), dma((1,)),
            dma((1,)), dma((1,)), dma((1,)), dma((1,)),
        ],
        compiler_params=pltpu.CompilerParams(
            collective_id=0, has_side_effects=True, vmem_limit_bytes=32 << 20
        ),
        cost_estimate=pl.CostEstimate(
            flops=2 * 1024 * 1664 * 4096, bytes_accessed=26 << 20, transcendentals=2 * 1024 * 1664
        ),
    )(
        pinned(activations[0]), pinned(out_grads[0]),
        pinned(weight_scale), pinned(moment_scale), pinned(second_scale),
        pinned(weight_code), pinned(moment_code), pinned(second_code),
    )
    peer_last = lax.ppermute(last, "rep", [(0, 1), (1, 0)])
    new_w, *rest = pl.pallas_call(
        store_kernel,
        out_shape=(
            shape((2048, 1664), BF16), shape((16, 13), F32),
            shape((1024, 1664), BF16), shape((8, 13), F32),
            shape((1024, 1664), BF16), shape((8, 13), F32),
        ),
        in_specs=[vmem] * 5,
        out_specs=(hbm,) * 6,
        scratch_shapes=[
            pltpu.VMEM((16, 13), F32), pltpu.VMEM((8, 13), F32), pltpu.VMEM((8, 13), F32),
            dma((4, 4)), dma((3,)),
        ],
        compiler_params=pltpu.CompilerParams(vmem_limit_bytes=8 << 20),
        cost_estimate=pl.CostEstimate(flops=0, bytes_accessed=26 << 20, transcendentals=0),
    )(*(pltpu.with_memory_space_constraint(x, pltpu.VMEM) for x in held))
    new_w = pl.pallas_call(
        last_kernel,
        out_shape=shape((2048, 1664), BF16),
        in_specs=[hbm, vmem],
        out_specs=hbm,
        input_output_aliases={0: 0},
        scratch_shapes=[dma((1,))],
        compiler_params=pltpu.CompilerParams(vmem_limit_bytes=8 << 20),
    )(new_w, peer_last)
    return (new_w, *rest)


def solution(mesh):
    return jax.shard_map(
        per_device,
        mesh=mesh,
        in_specs=(
            P("rep", "row", "col"),
            P("rep", "col", "row"),
            P(("col", "rep"), "row"),
            P(("col", "rep"), "row"),
            P(("col", "rep"), "row"),
            P(("col", "rep"), "row"),
            P(("col", "rep"), "row"),
            P(("col", "rep"), "row"),
        ),
        out_specs=(
            P("col", "row"),
            P("col", "row"),
            P(("col", "rep"), "row"),
            P(("col", "rep"), "row"),
            P(("col", "rep"), "row"),
            P(("col", "rep"), "row"),
        ),
        check_vma=False,
    )
```

```python
import functools

import jax
import jax.numpy as jnp
from jax import lax
from jax.experimental import pallas as pl
from jax.experimental.pallas import tpu as pltpu
from jax.sharding import PartitionSpec as P

MESH = pl.DeviceIdType.MESH
F32 = jnp.float32
BF16 = jnp.bfloat16
CHUNKS = 13
MOST = 12 * 128
BIAS_ONE = 1.0 - 0.9**10
BIAS_TWO = 1.0 - 0.95**10


def kernel(
    acts_in, grads, w_scale_in, m_scale_in, v_scale_in, w_code, m_code, v_code,
    W, peer_w, M, V, scales, last,
    acts, A, T, G, acc, new, peak, inv, w_scale, m_scale, v_scale,
    in_sem, own_sem, y_recv, z_recv, zf_recv, sib_recv,
    s1_recv, direct_recv, near_recv, far_recv, w_recv, sc_recv, a_send, g_send, w_send, sc_send,
):
    r, c, p = lax.axis_index("row"), lax.axis_index("col"), lax.axis_index("rep")
    yh, z, k = r // 8, (r // 2) % 4, r % 2
    q, yo = 1 - p, 1 - yh

    def at(yh_, z_, k_, c_, p_):
        return (yh_ * 8 + z_ * 2 + k_, c_, p_)

    partner = at(yh, z, k, c, q)
    other = at(yo, z, k, c, q)
    across = at(yo, z, k, c, p)
    sibling = at(yh, z, 1 - k, c, p)
    z_next, z_prev, z_far = (z + 1) % 4, (z + 3) % 4, (z + 2) % 4
    c_next, c_prev, c_far = (c + 1) % 4, (c + 3) % 4, (c + 2) % 4
    z_dev = (at(yh, z_next, k, c, p), at(yh, z_prev, k, c, p))
    x_dev = (at(yh, z, k, c_next, p), at(yh, z, k, c_prev, p))

    barrier = pltpu.get_barrier_semaphore()
    for device in (partner, other, across, sibling) + z_dev + x_dev:
        pl.semaphore_signal(barrier, inc=1, device_id=device, device_id_type=MESH)

    def remote(src, dst, send, recv, device):
        return pltpu.make_async_remote_copy(
            src_ref=src, dst_ref=dst, send_sem=send, recv_sem=recv,
            device_id=device, device_id_type=MESH,
        )

    def own_rows(part, c_):
        return pl.ds(pl.multiple_of(c_ * 1024 + part * 512, 512), 512)

    def cols(j):
        return pl.ds(pl.multiple_of(j * 128, 128), 128)

    def load_own(j):
        return pltpu.make_async_copy(grads.at[:, cols(j)], G.at[j, own_rows(p, c)], own_sem.at[0])

    load_acts = pltpu.make_async_copy(acts_in, acts, in_sem.at[3])
    load_acts.start()

    def start_own(j, carry):
        load_own(j).start()
        return carry

    lax.fori_loop(0, CHUNKS, start_own, 0)
    loads = [
        pltpu.make_async_copy(w_code, W, in_sem.at[0]),
        pltpu.make_async_copy(m_code, M, in_sem.at[1]),
        pltpu.make_async_copy(v_code, V, in_sem.at[2]),
        pltpu.make_async_copy(w_scale_in, w_scale, in_sem.at[4]),
        pltpu.make_async_copy(m_scale_in, m_scale, in_sem.at[5]),
        pltpu.make_async_copy(v_scale_in, v_scale, in_sem.at[6]),
    ]

    scales[0:24, :] = jnp.zeros((24, 128), F32)
    load_acts.wait()

    def idx(yh_, z_, k_, p_):
        return (yh_ * 2 + z_ // 2) * 8 + p_ * 4 + (z_ % 2) * 2 + k_

    mine = idx(yh, z, k, p)
    for i in range(8):
        A[mine, i * 128:(i + 1) * 128, :] = acts[:, pl.ds(pl.multiple_of(p * 1024 + i * 128, 128), 128)].T
        T[i * 128:(i + 1) * 128, :] = acts[:, pl.ds(pl.multiple_of(q * 1024 + i * 128, 128), 128)].T

    pl.semaphore_wait(barrier, 8)

    piece_yh = (yh, yh, yo, yo)
    piece_p = (p, q, q, p)

    def piece(i, z_, k_):
        return A.at[idx(piece_yh[i], z_, k_, piece_p[i])]

    def y_copy(i):
        src = A.at[mine] if i == 3 else T
        return remote(src, A.at[mine], a_send.at[0], y_recv.at[i], (None, partner, other, across)[i])

    def y_landed(i):
        got = piece(i, z, k)
        return remote(got, got, a_send.at[0], y_recv.at[i], (None, partner, other, across)[i])

    def z_copy(i, d):
        return remote(piece(i, z, k), piece(i, z, k), a_send.at[0], z_recv.at[i], z_dev[d])

    def z_landed(i):
        both = A.at[0:2]
        return remote(both, both, a_send.at[0], z_recv.at[i], z_dev[0])

    def zf_copy(i):
        d = i // 2
        got = piece(i, (z_prev, z_next)[d], k)
        return remote(got, got, a_send.at[0], zf_recv.at[i], z_dev[d])

    def zf_landed(i):
        got = piece(i, z_far, k)
        return remote(got, got, a_send.at[0], zf_recv.at[i], z_dev[i // 2])

    hops = (z, z_prev, z_next, z_far)

    def sib_copy(i, h):
        got = piece(i, hops[h], k)
        return remote(got, got, a_send.at[0], sib_recv.at[0], sibling)

    def sib_landed():
        every = A.at[0:16]
        return remote(every, every, a_send.at[0], sib_recv.at[0], sibling)

    def s1_copy(j):
        rows = G.at[j, own_rows(p, c)]
        return remote(rows, rows, g_send.at[0], s1_recv.at[j], partner)

    def s1_landed(j):
        rows = G.at[j, own_rows(q, c)]
        return remote(rows, rows, g_send.at[0], s1_recv.at[j], partner)

    def sx_copy(j, part, d):
        rows = G.at[j, own_rows((p, q)[part], c)]
        recv = direct_recv if part == d else near_recv
        return remote(rows, rows, g_send.at[0], recv.at[j], x_dev[d])

    def s4_copy(j, d):
        rows = G.at[j, own_rows((p, q)[d], (c_prev, c_next)[d])]
        return remote(rows, rows, g_send.at[0], far_recv.at[j], x_dev[d])

    def pair_landed(j, recv):
        both = G.at[j, 0:1024]
        return remote(both, both, g_send.at[0], recv.at[j], x_dev[0])

    def send_own(j):
        sx_copy(j, 0, 0).start()
        sx_copy(j, 0, 1).start()

    def send_partner(j):
        s1_landed(j).wait_recv()
        sx_copy(j, 1, 0).start()
        sx_copy(j, 1, 1).start()

    def send_direct(j):
        sx_copy(j, 0, 0).start()
        sx_copy(j, 1, 1).start()

    def send_near(j):
        sx_copy(j, 1, 0).start()
        sx_copy(j, 0, 1).start()

    def forward(j):
        pair_landed(j, direct_recv).wait_recv()
        s4_copy(j, 0).start()
        s4_copy(j, 1).start()

    def x_step(j):
        forward(j)

        @pl.when(j < 3)
        def _():
            send_partner(j + 3)

        @pl.when(jnp.logical_and(j > 3, j < CHUNKS - 2))
        def _():
            s1_landed(j + 2).wait_recv()
            send_direct(j + 2)

        @pl.when(jnp.logical_and(j > 3, j < CHUNKS - 3))
        def _():
            send_near(j + 2)

        @pl.when(j == CHUNKS - 2)
        def _():
            send_near(j + 1)

    def relay(i):
        z_landed(i).wait_recv()
        zf_copy(i).start()
        sib_copy(i, 1).start()
        sib_copy(i, 2).start()

    def spread(i):
        y_landed(i).wait_recv()
        z_copy(i, 0).start()
        z_copy(i, 1).start()
        sib_copy(i, 0).start()

    def finish(i):
        zf_landed(i).wait_recv()
        sib_copy(i, 3).start()

    for i in (1, 2, 3):
        y_copy(i).start()
    own = G.at[:, own_rows(p, c)]
    pltpu.make_async_copy(own, own, own_sem.at[0]).wait()

    send_own(0)
    z_copy(0, 0).start()
    z_copy(0, 1).start()

    def start_own_sends(j, carry):
        send_own(j)
        return carry

    lax.fori_loop(1, 6, start_own_sends, 0)

    def start_s1(j, carry):
        s1_copy(j).start()
        return carry

    lax.fori_loop(0, CHUNKS, start_s1, 0)
    sib_copy(0, 0).start()
    for load in loads:
        load.start()

    spread(1)
    spread(2)
    relay(0)
    spread(3)
    send_partner(0)
    relay(1)
    send_partner(1)
    relay(2)
    send_partner(2)
    x_step(0)
    x_step(1)
    x_step(2)
    relay(3)
    x_step(3)
    finish(0)
    finish(2)
    x_step(4)
    finish(1)
    finish(3)
    for load in loads:
        load.wait()
    sib_landed().wait_recv()

    lane = lax.broadcasted_iota(jnp.int32, (24, 128), 1)

    def w_copy(j):
        return remote(W.at[:, cols(j)], peer_w.at[:, cols(j)], w_send.at[0], w_recv.at[0], partner)

    sc_copy = remote(scales.at[0:8], scales.at[24:32], sc_send.at[0], sc_recv.at[0], partner)

    keep_last = pltpu.make_async_copy(W.at[:, MOST:], last, in_sem.at[3])

    def product(j, c_):
        left = jnp.concatenate([A[c_ * 8 + i] for i in range(8)], axis=1)
        right = G[j, pl.ds(pl.multiple_of(c_ * 1024, 1024), 1024), :]
        return jnp.dot(left, right, preferred_element_type=F32)

    def chunk(j, carry):
        @pl.when(jnp.logical_or(j == 0, j == 3))
        def _():
            x_step(5 + j // 2)

        @pl.when(jnp.logical_or(j == 5, jnp.logical_and(j > 6, j < CHUNKS - 1)))
        def _():
            x_step(jnp.where(j == 5, 7, j + 1))

        pair_landed(j, near_recv).wait_recv()
        acc[...] = product(j, c) + product(j, c_prev) + product(j, c_next)
        pair_landed(j, far_recv).wait_recv()
        acc[...] += product(j, c_far)

        def update(d, carry):
            rows = pl.ds(pl.multiple_of(d * 128, 128), 128)
            g = acc[rows, :]
            weight = W[rows, cols(j)].astype(F32) * w_scale[d, j]
            moment = M[rows, cols(j)].astype(F32) * m_scale[d, j]
            second = V[rows, cols(j)].astype(F32) * v_scale[d, j]
            moment1 = 0.9 * moment + 0.1 * g
            second1 = 0.95 * second + 0.05 * (g * g)
            u = second1 * (1.0 / BIAS_TWO)
            denom = u * lax.rsqrt(u) + 1e-08
            weight1 = weight - 0.01 * ((moment1 * (1.0 / BIAS_ONE)) / denom + 0.1 * weight)
            for n, value in enumerate((weight1, moment1, second1)):
                new[n, rows, :] = value
                peak[n * 8 + d] = jnp.max(jnp.abs(value).reshape(16, 8, 128), axis=0)
            return carry

        lax.fori_loop(0, 8, update, 0)
        scale = jnp.max(jnp.max(peak[...], axis=1), axis=1, keepdims=True) + 1e-06
        scale = jnp.broadcast_to(scale, (24, 128))
        scales[0:24, :] = jnp.where(lane == j, scale, scales[0:24, :])
        inv[...] = 1.0 / scale

        @pl.when(j == CHUNKS - 1)
        def _():
            sc_copy.start()

        def encode(d, carry):
            rows = pl.ds(pl.multiple_of(d * 128, 128), 128)
            for n, out in enumerate((W, M, V)):
                out[rows, cols(j)] = (new[n, rows, :] * inv[pl.ds(n * 8 + d, 1), :]).astype(BF16)
            return carry

        lax.fori_loop(0, 8, encode, 0)
        @pl.when(j < CHUNKS - 1)
        def _():
            w_copy(j).start()

        @pl.when(j == CHUNKS - 1)
        def _():
            keep_last.start()

        return carry

    lax.fori_loop(0, CHUNKS, chunk, 0)

    sent = A.at[0:31]
    remote(sent, sent, a_send.at[0], sib_recv.at[0], sibling).wait_send()
    sent = G.at[:, 0:3584]
    remote(sent, sent, g_send.at[0], s1_recv.at[0], partner).wait_send()
    keep_last.wait()
    codes = remote(W.at[:, :MOST], peer_w.at[:, :MOST], w_send.at[0], w_recv.at[0], partner)
    codes.wait_send()
    codes.wait_recv()
    sc_copy.wait()


def store_kernel(W, peer_w, M, V, scales, w_out, ws_out, m_out, ms_out, v_out, vs_out, ws, ms, vs, sem, sc_sem):
    p = lax.axis_index("rep")
    q = 1 - p
    copies = []
    for n in range(1):
        rows = pl.ds(n * 1024, 1024)
        here = pl.ds(pl.multiple_of(p * 1024 + n * 1024, 1024), 1024)
        there = pl.ds(pl.multiple_of(q * 1024 + n * 1024, 1024), 1024)
        copies += [
            pltpu.make_async_copy(W.at[rows], w_out.at[here], sem.at[0, n]),
            pltpu.make_async_copy(peer_w.at[rows, :MOST], w_out.at[there, :MOST], sem.at[1, n]),
            pltpu.make_async_copy(M.at[rows], m_out.at[rows], sem.at[2, n]),
            pltpu.make_async_copy(V.at[rows], v_out.at[rows], sem.at[3, n]),
        ]
    for copy in copies:
        copy.start()
    ws[pl.ds(pl.multiple_of(p * 8, 8), 8), :] = scales[0:8, :CHUNKS]
    ws[pl.ds(pl.multiple_of(q * 8, 8), 8), :] = scales[24:32, :CHUNKS]
    ms[...] = scales[8:16, :CHUNKS]
    vs[...] = scales[16:24, :CHUNKS]
    for n, (src, dst) in enumerate(((ws, ws_out), (ms, ms_out), (vs, vs_out))):
        copies.append(pltpu.make_async_copy(src, dst, sc_sem.at[n]))
        copies[-1].start()
    for copy in copies:
        copy.wait()


def last_kernel(_, peer_last, w_out, sem):
    there = pl.ds(pl.multiple_of((1 - lax.axis_index("rep")) * 1024, 1024), 1024)
    copy = pltpu.make_async_copy(peer_last, w_out.at[there, MOST:], sem.at[0])
    copy.start()
    copy.wait()


def per_device(
    activations, out_grads, weight_code, weight_scale,
    moment_code, moment_scale, second_code, second_scale,
):
    vmem = pl.BlockSpec(memory_space=pltpu.VMEM)
    hbm = pl.BlockSpec(memory_space=pl.ANY)
    dma = pltpu.SemaphoreType.DMA
    shape = jax.ShapeDtypeStruct
    pinned = functools.partial(pltpu.with_memory_space_constraint, memory_space=pltpu.HBM)
    codes = pltpu.VMEM((1024, 1664), BF16)
    *held, last = pl.pallas_call(
        kernel,
        out_shape=(codes, codes, codes, codes, pltpu.VMEM((32, 128), F32), shape((1024, 128), BF16)),
        in_specs=[hbm] * 8,
        out_specs=(vmem,) * 5 + (hbm,),
        scratch_shapes=[
            pltpu.VMEM((128, 2048), BF16),
            pltpu.VMEM((32, 1024, 128), BF16),
            pltpu.VMEM((1024, 128), BF16),
            pltpu.VMEM((CHUNKS, 4096, 128), BF16),
            pltpu.VMEM((1024, 128), F32),
            pltpu.VMEM((3, 1024, 128), F32),
            pltpu.VMEM((24, 8, 128), F32),
            pltpu.VMEM((24, 128), F32),
            pltpu.SMEM((8, 13), F32),
            pltpu.SMEM((8, 13), F32),
            pltpu.SMEM((8, 13), F32),
            dma((7,)), dma((1,)), dma((4,)), dma((4,)), dma((4,)), dma((1,)),
            dma((CHUNKS,)), dma((CHUNKS,)), dma((CHUNKS,)), dma((CHUNKS,)), dma((1,)), dma((1,)),
            dma((1,)), dma((1,)), dma((1,)), dma((1,)),
        ],
        compiler_params=pltpu.CompilerParams(
            collective_id=0, has_side_effects=True, vmem_limit_bytes=32 << 20
        ),
        cost_estimate=pl.CostEstimate(
            flops=2 * 1024 * 1664 * 4096, bytes_accessed=26 << 20, transcendentals=2 * 1024 * 1664
        ),
    )(
        pinned(activations[0]), pinned(out_grads[0]),
        pinned(weight_scale), pinned(moment_scale), pinned(second_scale),
        pinned(weight_code), pinned(moment_code), pinned(second_code),
    )
    peer_last = lax.ppermute(last, "rep", [(0, 1), (1, 0)])
    new_w, *rest = pl.pallas_call(
        store_kernel,
        out_shape=(
            shape((2048, 1664), BF16), shape((16, 13), F32),
            shape((1024, 1664), BF16), shape((8, 13), F32),
            shape((1024, 1664), BF16), shape((8, 13), F32),
        ),
        in_specs=[vmem] * 5,
        out_specs=(hbm,) * 6,
        scratch_shapes=[
            pltpu.VMEM((16, 13), F32), pltpu.VMEM((8, 13), F32), pltpu.VMEM((8, 13), F32),
            dma((4, 1)), dma((3,)),
        ],
        compiler_params=pltpu.CompilerParams(vmem_limit_bytes=8 << 20),
        cost_estimate=pl.CostEstimate(flops=0, bytes_accessed=26 << 20, transcendentals=0),
    )(*(pltpu.with_memory_space_constraint(x, pltpu.VMEM) for x in held))
    new_w = pl.pallas_call(
        last_kernel,
        out_shape=shape((2048, 1664), BF16),
        in_specs=[hbm, vmem],
        out_specs=hbm,
        input_output_aliases={0: 0},
        scratch_shapes=[dma((1,))],
        compiler_params=pltpu.CompilerParams(vmem_limit_bytes=8 << 20),
    )(new_w, peer_last)
    return (new_w, *rest)


def solution(mesh):
    return jax.shard_map(
        per_device,
        mesh=mesh,
        in_specs=(
            P("rep", "row", "col"),
            P("rep", "col", "row"),
            P(("col", "rep"), "row"),
            P(("col", "rep"), "row"),
            P(("col", "rep"), "row"),
            P(("col", "rep"), "row"),
            P(("col", "rep"), "row"),
            P(("col", "rep"), "row"),
        ),
        out_specs=(
            P("col", "row"),
            P("col", "row"),
            P(("col", "rep"), "row"),
            P(("col", "rep"), "row"),
            P(("col", "rep"), "row"),
            P(("col", "rep"), "row"),
        ),
        check_vma=False,
    )
```

```python
import functools

import jax
import jax.numpy as jnp
from jax import lax
from jax.experimental import pallas as pl
from jax.experimental.pallas import tpu as pltpu
from jax.sharding import PartitionSpec as P

MESH = pl.DeviceIdType.MESH
F32 = jnp.float32
BF16 = jnp.bfloat16
CHUNKS = 13
MOST = 12 * 128
BIAS_ONE = 1.0 - 0.9**10
BIAS_TWO = 1.0 - 0.95**10


def kernel(
    acts_in, grads, w_scale_in, m_scale_in, v_scale_in, w_code, m_code, v_code,
    W, peer_w, M, V, scales, last,
    acts, A, T, G, acc, new, peak, inv, w_scale, m_scale, v_scale,
    in_sem, own_sem, y_recv, z_recv, zf_recv, sib_recv,
    s1_recv, direct_recv, near_recv, far_recv, w_recv, sc_recv, a_send, g_send, w_send, sc_send,
):
    r, c, p = lax.axis_index("row"), lax.axis_index("col"), lax.axis_index("rep")
    yh, z, k = r // 8, (r // 2) % 4, r % 2
    q, yo = 1 - p, 1 - yh

    def at(yh_, z_, k_, c_, p_):
        return (yh_ * 8 + z_ * 2 + k_, c_, p_)

    partner = at(yh, z, k, c, q)
    other = at(yo, z, k, c, q)
    across = at(yo, z, k, c, p)
    sibling = at(yh, z, 1 - k, c, p)
    z_next, z_prev, z_far = (z + 1) % 4, (z + 3) % 4, (z + 2) % 4
    c_next, c_prev, c_far = (c + 1) % 4, (c + 3) % 4, (c + 2) % 4
    z_dev = (at(yh, z_next, k, c, p), at(yh, z_prev, k, c, p))
    x_dev = (at(yh, z, k, c_next, p), at(yh, z, k, c_prev, p))

    barrier = pltpu.get_barrier_semaphore()
    for device in (partner, other, across, sibling) + z_dev + x_dev:
        pl.semaphore_signal(barrier, inc=1, device_id=device, device_id_type=MESH)

    def remote(src, dst, send, recv, device):
        return pltpu.make_async_remote_copy(
            src_ref=src, dst_ref=dst, send_sem=send, recv_sem=recv,
            device_id=device, device_id_type=MESH,
        )

    def own_rows(part, c_):
        return pl.ds(pl.multiple_of(c_ * 1024 + part * 512, 512), 512)

    def cols(j):
        return pl.ds(pl.multiple_of(j * 128, 128), 128)

    def load_own(j):
        return pltpu.make_async_copy(grads.at[:, cols(j)], G.at[j, own_rows(p, c)], own_sem.at[0])

    load_acts = pltpu.make_async_copy(acts_in, acts, in_sem.at[3])
    load_acts.start()

    def start_own(j, carry):
        load_own(j).start()
        return carry

    lax.fori_loop(0, CHUNKS, start_own, 0)
    loads = [
        pltpu.make_async_copy(w_code, W, in_sem.at[0]),
        pltpu.make_async_copy(m_code, M, in_sem.at[1]),
        pltpu.make_async_copy(v_code, V, in_sem.at[2]),
        pltpu.make_async_copy(w_scale_in, w_scale, in_sem.at[4]),
        pltpu.make_async_copy(m_scale_in, m_scale, in_sem.at[5]),
        pltpu.make_async_copy(v_scale_in, v_scale, in_sem.at[6]),
    ]

    scales[0:24, :] = jnp.zeros((24, 128), F32)
    load_acts.wait()

    def idx(yh_, z_, k_, p_):
        return (yh_ * 2 + z_ // 2) * 8 + p_ * 4 + (z_ % 2) * 2 + k_

    mine = idx(yh, z, k, p)
    for i in range(8):
        A[mine, i * 128:(i + 1) * 128, :] = acts[:, pl.ds(pl.multiple_of(p * 1024 + i * 128, 128), 128)].T
        T[i * 128:(i + 1) * 128, :] = acts[:, pl.ds(pl.multiple_of(q * 1024 + i * 128, 128), 128)].T

    pl.semaphore_wait(barrier, 8)

    piece_yh = (yh, yh, yo, yo)
    piece_p = (p, q, q, p)

    def piece(i, z_, k_):
        return A.at[idx(piece_yh[i], z_, k_, piece_p[i])]

    def y_copy(i):
        src = A.at[mine] if i == 3 else T
        return remote(src, A.at[mine], a_send.at[0], y_recv.at[i], (None, partner, other, across)[i])

    def y_landed(i):
        got = piece(i, z, k)
        return remote(got, got, a_send.at[0], y_recv.at[i], (None, partner, other, across)[i])

    def z_copy(i, d):
        return remote(piece(i, z, k), piece(i, z, k), a_send.at[0], z_recv.at[i], z_dev[d])

    def z_landed(i):
        both = A.at[0:2]
        return remote(both, both, a_send.at[0], z_recv.at[i], z_dev[0])

    def zf_copy(i):
        d = i // 2
        got = piece(i, (z_prev, z_next)[d], k)
        return remote(got, got, a_send.at[0], zf_recv.at[i], z_dev[d])

    def zf_landed(i):
        got = piece(i, z_far, k)
        return remote(got, got, a_send.at[0], zf_recv.at[i], z_dev[i // 2])

    hops = (z, z_prev, z_next, z_far)

    def sib_copy(i, h):
        got = piece(i, hops[h], k)
        return remote(got, got, a_send.at[0], sib_recv.at[0], sibling)

    def sib_landed():
        every = A.at[0:16]
        return remote(every, every, a_send.at[0], sib_recv.at[0], sibling)

    def s1_copy(j):
        rows = G.at[j, own_rows(p, c)]
        return remote(rows, rows, g_send.at[0], s1_recv.at[j], partner)

    def s1_landed(j):
        rows = G.at[j, own_rows(q, c)]
        return remote(rows, rows, g_send.at[0], s1_recv.at[j], partner)

    def sx_copy(j, part, d):
        rows = G.at[j, own_rows((p, q)[part], c)]
        recv = direct_recv if part == d else near_recv
        return remote(rows, rows, g_send.at[0], recv.at[j], x_dev[d])

    def s4_copy(j, d):
        rows = G.at[j, own_rows((p, q)[d], (c_prev, c_next)[d])]
        return remote(rows, rows, g_send.at[0], far_recv.at[j], x_dev[d])

    def pair_landed(j, recv):
        both = G.at[j, 0:1024]
        return remote(both, both, g_send.at[0], recv.at[j], x_dev[0])

    def send_own(j):
        sx_copy(j, 0, 0).start()
        sx_copy(j, 0, 1).start()

    def send_partner(j):
        s1_landed(j).wait_recv()
        sx_copy(j, 1, 0).start()
        sx_copy(j, 1, 1).start()

    def send_direct(j):
        sx_copy(j, 0, 0).start()
        sx_copy(j, 1, 1).start()

    def send_near(j):
        sx_copy(j, 1, 0).start()
        sx_copy(j, 0, 1).start()

    def forward(j):
        pair_landed(j, direct_recv).wait_recv()
        s4_copy(j, 0).start()
        s4_copy(j, 1).start()

    def x_step(j):
        forward(j)

        @pl.when(j < 3)
        def _():
            send_partner(j + 3)

        @pl.when(jnp.logical_and(j > 3, j < CHUNKS - 2))
        def _():
            s1_landed(j + 2).wait_recv()
            send_direct(j + 2)

        @pl.when(jnp.logical_and(j > 3, j < CHUNKS - 3))
        def _():
            send_near(j + 2)

        @pl.when(j == CHUNKS - 2)
        def _():
            send_near(j + 1)

    def relay(i):
        z_landed(i).wait_recv()
        zf_copy(i).start()
        sib_copy(i, 1).start()
        sib_copy(i, 2).start()

    def spread(i):
        y_landed(i).wait_recv()
        z_copy(i, 0).start()
        z_copy(i, 1).start()
        sib_copy(i, 0).start()

    def finish(i):
        zf_landed(i).wait_recv()
        sib_copy(i, 3).start()

    for i in (1, 3, 2):
        y_copy(i).start()
    own = G.at[:, own_rows(p, c)]
    pltpu.make_async_copy(own, own, own_sem.at[0]).wait()

    send_own(0)
    z_copy(0, 0).start()
    z_copy(0, 1).start()

    def start_own_sends(j, carry):
        send_own(j)
        return carry

    lax.fori_loop(1, 6, start_own_sends, 0)

    def start_s1(j, carry):
        s1_copy(j).start()
        return carry

    lax.fori_loop(0, CHUNKS, start_s1, 0)
    sib_copy(0, 0).start()
    for load in loads:
        load.start()

    spread(1)
    spread(2)
    relay(0)
    spread(3)
    send_partner(0)
    relay(1)
    send_partner(1)
    relay(2)
    send_partner(2)
    x_step(0)
    x_step(1)
    x_step(2)
    relay(3)
    x_step(3)
    finish(0)
    finish(2)
    x_step(4)
    finish(1)
    finish(3)
    for load in loads:
        load.wait()
    sib_landed().wait_recv()

    lane = lax.broadcasted_iota(jnp.int32, (24, 128), 1)

    def w_copy(j):
        return remote(W.at[:, cols(j)], peer_w.at[:, cols(j)], w_send.at[0], w_recv.at[0], partner)

    sc_copy = remote(scales.at[0:8], scales.at[24:32], sc_send.at[0], sc_recv.at[0], partner)

    keep_last = pltpu.make_async_copy(W.at[:, MOST:], last, in_sem.at[3])

    def product(j, c_):
        left = jnp.concatenate([A[c_ * 8 + i] for i in range(8)], axis=1)
        right = G[j, pl.ds(pl.multiple_of(c_ * 1024, 1024), 1024), :]
        return jnp.dot(left, right, preferred_element_type=F32)

    def chunk(j, carry):
        @pl.when(jnp.logical_or(j == 0, j == 3))
        def _():
            x_step(5 + j // 2)

        @pl.when(jnp.logical_or(j == 5, jnp.logical_and(j > 6, j < CHUNKS - 1)))
        def _():
            x_step(jnp.where(j == 5, 7, j + 1))

        pair_landed(j, near_recv).wait_recv()
        acc[...] = product(j, c) + product(j, c_prev) + product(j, c_next)
        pair_landed(j, far_recv).wait_recv()
        acc[...] += product(j, c_far)

        def update(d, carry):
            rows = pl.ds(pl.multiple_of(d * 128, 128), 128)
            g = acc[rows, :]
            weight = W[rows, cols(j)].astype(F32) * w_scale[d, j]
            moment = M[rows, cols(j)].astype(F32) * m_scale[d, j]
            second = V[rows, cols(j)].astype(F32) * v_scale[d, j]
            moment1 = 0.9 * moment + 0.1 * g
            second1 = 0.95 * second + 0.05 * (g * g)
            u = second1 * (1.0 / BIAS_TWO)
            denom = u * lax.rsqrt(u) + 1e-08
            weight1 = weight - 0.01 * ((moment1 * (1.0 / BIAS_ONE)) / denom + 0.1 * weight)
            for n, value in enumerate((weight1, moment1, second1)):
                new[n, rows, :] = value
                peak[n * 8 + d] = jnp.max(jnp.abs(value).reshape(16, 8, 128), axis=0)
            return carry

        lax.fori_loop(0, 8, update, 0)
        scale = jnp.max(jnp.max(peak[...], axis=1), axis=1, keepdims=True) + 1e-06
        scale = jnp.broadcast_to(scale, (24, 128))
        scales[0:24, :] = jnp.where(lane == j, scale, scales[0:24, :])
        inv[...] = 1.0 / scale

        @pl.when(j == CHUNKS - 1)
        def _():
            sc_copy.start()

        def encode(d, carry):
            rows = pl.ds(pl.multiple_of(d * 128, 128), 128)
            for n, out in enumerate((W, M, V)):
                out[rows, cols(j)] = (new[n, rows, :] * inv[pl.ds(n * 8 + d, 1), :]).astype(BF16)
            return carry

        lax.fori_loop(0, 8, encode, 0)
        @pl.when(j < CHUNKS - 1)
        def _():
            w_copy(j).start()

        @pl.when(j == CHUNKS - 1)
        def _():
            keep_last.start()

        return carry

    lax.fori_loop(0, CHUNKS, chunk, 0)

    sent = A.at[0:31]
    remote(sent, sent, a_send.at[0], sib_recv.at[0], sibling).wait_send()
    sent = G.at[:, 0:3584]
    remote(sent, sent, g_send.at[0], s1_recv.at[0], partner).wait_send()
    keep_last.wait()
    codes = remote(W.at[:, :MOST], peer_w.at[:, :MOST], w_send.at[0], w_recv.at[0], partner)
    codes.wait_send()
    codes.wait_recv()
    sc_copy.wait()


def store_kernel(W, peer_w, M, V, scales, w_out, ws_out, m_out, ms_out, v_out, vs_out, ws, ms, vs, sem, sc_sem):
    p = lax.axis_index("rep")
    q = 1 - p
    copies = []
    for n in range(1):
        rows = pl.ds(n * 1024, 1024)
        here = pl.ds(pl.multiple_of(p * 1024 + n * 1024, 1024), 1024)
        there = pl.ds(pl.multiple_of(q * 1024 + n * 1024, 1024), 1024)
        copies += [
            pltpu.make_async_copy(W.at[rows], w_out.at[here], sem.at[0, n]),
            pltpu.make_async_copy(peer_w.at[rows, :MOST], w_out.at[there, :MOST], sem.at[1, n]),
            pltpu.make_async_copy(M.at[rows], m_out.at[rows], sem.at[2, n]),
            pltpu.make_async_copy(V.at[rows], v_out.at[rows], sem.at[3, n]),
        ]
    for copy in copies:
        copy.start()
    ws[pl.ds(pl.multiple_of(p * 8, 8), 8), :] = scales[0:8, :CHUNKS]
    ws[pl.ds(pl.multiple_of(q * 8, 8), 8), :] = scales[24:32, :CHUNKS]
    ms[...] = scales[8:16, :CHUNKS]
    vs[...] = scales[16:24, :CHUNKS]
    for n, (src, dst) in enumerate(((ws, ws_out), (ms, ms_out), (vs, vs_out))):
        copies.append(pltpu.make_async_copy(src, dst, sc_sem.at[n]))
        copies[-1].start()
    for copy in copies:
        copy.wait()


def last_kernel(_, peer_last, w_out, sem):
    there = pl.ds(pl.multiple_of((1 - lax.axis_index("rep")) * 1024, 1024), 1024)
    copy = pltpu.make_async_copy(peer_last, w_out.at[there, MOST:], sem.at[0])
    copy.start()
    copy.wait()


def per_device(
    activations, out_grads, weight_code, weight_scale,
    moment_code, moment_scale, second_code, second_scale,
):
    vmem = pl.BlockSpec(memory_space=pltpu.VMEM)
    hbm = pl.BlockSpec(memory_space=pl.ANY)
    dma = pltpu.SemaphoreType.DMA
    shape = jax.ShapeDtypeStruct
    pinned = functools.partial(pltpu.with_memory_space_constraint, memory_space=pltpu.HBM)
    codes = pltpu.VMEM((1024, 1664), BF16)
    *held, last = pl.pallas_call(
        kernel,
        out_shape=(codes, codes, codes, codes, pltpu.VMEM((32, 128), F32), shape((1024, 128), BF16)),
        in_specs=[hbm] * 8,
        out_specs=(vmem,) * 5 + (hbm,),
        scratch_shapes=[
            pltpu.VMEM((128, 2048), BF16),
            pltpu.VMEM((32, 1024, 128), BF16),
            pltpu.VMEM((1024, 128), BF16),
            pltpu.VMEM((CHUNKS, 4096, 128), BF16),
            pltpu.VMEM((1024, 128), F32),
            pltpu.VMEM((3, 1024, 128), F32),
            pltpu.VMEM((24, 8, 128), F32),
            pltpu.VMEM((24, 128), F32),
            pltpu.SMEM((8, 13), F32),
            pltpu.SMEM((8, 13), F32),
            pltpu.SMEM((8, 13), F32),
            dma((7,)), dma((1,)), dma((4,)), dma((4,)), dma((4,)), dma((1,)),
            dma((CHUNKS,)), dma((CHUNKS,)), dma((CHUNKS,)), dma((CHUNKS,)), dma((1,)), dma((1,)),
            dma((1,)), dma((1,)), dma((1,)), dma((1,)),
        ],
        compiler_params=pltpu.CompilerParams(
            collective_id=0, has_side_effects=True, vmem_limit_bytes=32 << 20
        ),
        cost_estimate=pl.CostEstimate(
            flops=2 * 1024 * 1664 * 4096, bytes_accessed=26 << 20, transcendentals=2 * 1024 * 1664
        ),
    )(
        pinned(activations[0]), pinned(out_grads[0]),
        pinned(weight_scale), pinned(moment_scale), pinned(second_scale),
        pinned(weight_code), pinned(moment_code), pinned(second_code),
    )
    peer_last = lax.ppermute(last, "rep", [(0, 1), (1, 0)])
    new_w, *rest = pl.pallas_call(
        store_kernel,
        out_shape=(
            shape((2048, 1664), BF16), shape((16, 13), F32),
            shape((1024, 1664), BF16), shape((8, 13), F32),
            shape((1024, 1664), BF16), shape((8, 13), F32),
        ),
        in_specs=[vmem] * 5,
        out_specs=(hbm,) * 6,
        scratch_shapes=[
            pltpu.VMEM((16, 13), F32), pltpu.VMEM((8, 13), F32), pltpu.VMEM((8, 13), F32),
            dma((4, 1)), dma((3,)),
        ],
        compiler_params=pltpu.CompilerParams(vmem_limit_bytes=8 << 20),
        cost_estimate=pl.CostEstimate(flops=0, bytes_accessed=26 << 20, transcendentals=0),
    )(*(pltpu.with_memory_space_constraint(x, pltpu.VMEM) for x in held))
    new_w = pl.pallas_call(
        last_kernel,
        out_shape=shape((2048, 1664), BF16),
        in_specs=[hbm, vmem],
        out_specs=hbm,
        input_output_aliases={0: 0},
        scratch_shapes=[dma((1,))],
        compiler_params=pltpu.CompilerParams(vmem_limit_bytes=8 << 20),
    )(new_w, peer_last)
    return (new_w, *rest)


def solution(mesh):
    return jax.shard_map(
        per_device,
        mesh=mesh,
        in_specs=(
            P("rep", "row", "col"),
            P("rep", "col", "row"),
            P(("col", "rep"), "row"),
            P(("col", "rep"), "row"),
            P(("col", "rep"), "row"),
            P(("col", "rep"), "row"),
            P(("col", "rep"), "row"),
            P(("col", "rep"), "row"),
        ),
        out_specs=(
            P("col", "row"),
            P("col", "row"),
            P(("col", "rep"), "row"),
            P(("col", "rep"), "row"),
            P(("col", "rep"), "row"),
            P(("col", "rep"), "row"),
        ),
        check_vma=False,
    )
```
